128 devices in a mesh: chan: 8 (over x, y_hi), facet: 16 (over y_lo, z, core).
Axes of the slice: x: 4, y: 4 (y_hi: 2, y_lo: 2; y = y_hi * 2 + y_lo), z: 4, core: 2. Of those that a mesh axis runs over, the one named last changes fastest.
Arguments:
- image: float32 [8, 2048, 2048], P(None, 'facet', 'chan'), may hold values from 0 to 1
- lowrank_dual: float32 [8, 2048, 2048], P(None, 'facet', 'chan'), may hold values from -6 to 6
- wavelet_dual: float32 [8, 4096, 4096], P(None, 'facet', 'chan'), may hold values from -6 to 6
- data_dual: float32 [2, 8, 512, 2048], P(None, 'chan', None, 'facet'), may hold values from -6 to 6
- observed: float32 [2, 8, 512, 2048], P(None, 'chan', None, 'facet'), may hold values from -6 to 6
- kernel_weights: bfloat16 [8, 512, 2048], P('chan', None, 'facet'), may hold values from 0.25 to 2
- analysis_matrix: bfloat16 [256, 256], replicated, may hold values from -0.375 to 0.375
- block_rows: int32 [8, 16, 4], P('chan', 'facet'), may hold values from 0 to 15, as said below
- intersection_widths: int32 [16, 16], P('facet', 'chan'), may hold values from 16 to 64
- ball_radii: float32 [8, 16], P('chan', 'facet'), may hold values from 230.4 to 614.4
Outputs:
- image_next: float32 [8, 2048, 2048], P(None, 'facet', 'chan')
- lowrank_next: float32 [8, 2048, 2048], P(None, 'facet', 'chan')
- wavelet_next: float32 [8, 4096, 4096], P(None, 'facet', 'chan')
- data_next: float32 [2, 8, 512, 2048], P(None, 'chan', None, 'facet')
The draws below stay inside these ranges and needn't reach their ends.
Inputs may be any that keep to these rules, and one draw needn't show every extreme that they name: `block_rows`: for each channel and column block the 4 row blocks are distinct.
All inputs are finite; a program needn't handle non-finite values.
Results may differ from the reference program's by a relative error of at most 0.0062.
Values may be sent and summed in bfloat16 or wider, within the bound.
A program may use at most 128 MiB of HBM per device.

```python
import math
import jax
import jax.numpy as jnp
from jax import lax

N = 2048
FACETS = 16
FS = 128
HALO = 64
E = 256
BLK = 128
NB = 16
R = 4
C = 8


def draw_block_rows(key, part):
    key = jax.random.fold_in(key, 11)
    scores = jax.random.randint(key, (C, NB, NB), 0, 1 << 20)
    scores = scores * NB + jnp.arange(NB, dtype=jnp.int32)
    ceiling = (1 << 20) * NB + NB
    scores = scores.at[0, 0, 0].set(ceiling + 1)
    scores = scores.at[0, 0, NB - 1].set(ceiling + 2)
    return lax.top_k(scores, R)[1].astype(jnp.int32)


def draw_intersection_widths(key, part):
    key = jax.random.fold_in(key, 12)
    key_values, key_highest, key_lowest = jax.random.split(key, 3)
    widths = jax.random.randint(key_values, (FACETS, FACETS), HALO // 4, HALO + 1)
    places = jnp.arange(FACETS * FACETS, dtype=jnp.int32).reshape(FACETS, FACETS)
    highest_at = jax.random.randint(key_highest, (), 0, FACETS * FACETS)
    lowest_at = jax.random.randint(key_lowest, (), 0, FACETS * FACETS)
    widths = jnp.where(places == lowest_at, HALO // 4, widths)
    return jnp.where(places == highest_at, HALO, widths).astype(jnp.int32)


def level_of(key, extent, pieces, low, top_value):
    factor_of, own = 1.0, jax.random.fold_in(key, 6)
    for position, parts in pieces:
        steps = jnp.exp(jax.random.uniform(jax.random.fold_in(own, position), (parts,), jnp.float32, low / len(pieces), top_value / len(pieces)))
        factor_of = factor_of * jnp.repeat(steps, extent[position] // parts).reshape([-1 if axis == position else 1 for axis in range(len(extent))])
    return factor_of


def bell_draw(key, shape, deviation, most, pieces=(), held_as=jnp.bfloat16):
    level = level_of(key, shape, pieces, -0.22, 0.18) if pieces else 1.0
    entries = jax.random.normal(key, shape, jnp.float32) * deviation * level
    return jnp.minimum(jnp.maximum(entries, -most), most).astype(held_as)


def setup_inputs(seed: int = 0) -> dict:
    key_list = jax.random.split(jax.random.key(seed), 11)
    return {
        "image": jnp.clip(1.0 * jax.random.uniform(key_list[0], (C, N, N), jnp.float32) ** level_of(key_list[0], (C, N, N), ((1, 16), (2, 8)), -0.2, 0.2), 0.0, 1.0),
        "lowrank_dual": bell_draw(key_list[1], (C, N, N), 1.0, 6.0, ((1, 16), (2, 8)), jnp.float32),
        "wavelet_dual": bell_draw(key_list[2], (C, FACETS * E, FACETS * E), 1.0, 6.0, ((1, 16), (2, 8)), jnp.float32),
        "data_dual": bell_draw(key_list[3], (2, C, R * BLK, N), 1.0, 6.0, ((1, 8), (3, 16)), jnp.float32),
        "observed": bell_draw(key_list[4], (2, C, R * BLK, N), 1.0, 6.0, ((1, 8), (3, 16)), jnp.float32),
        "kernel_weights": jnp.clip(jnp.exp(math.log(2.0) - 2.0794415 * jax.random.uniform(key_list[5], (C, R * BLK, N), jnp.float32) ** level_of(key_list[5], (C, R * BLK, N), ((0, 8), (2, 16)), -0.2, 0.2)), 0.25, 2.0).astype(jnp.bfloat16),
        "analysis_matrix": bell_draw(key_list[6], (E, E), E ** -0.5, 0.375),
        "block_rows": draw_block_rows(jax.random.fold_in(key_list[10], 71), 0),
        "intersection_widths": draw_intersection_widths(jax.random.fold_in(key_list[10], 71), 0),
        "ball_radii": jnp.clip(jnp.exp(math.log(614.4) - 0.9808293 * jax.random.uniform(key_list[9], (C, NB), jnp.float32) ** level_of(key_list[9], (C, NB), ((0, 8), (1, 16)), -0.2, 0.2)), 230.4, 614.4),
    }


step_size = 0.5
clip_bound = 1.5
shrink_ratio = 0.5
tiny_value = 1e-06

def dft_rows(row_index):
    columns = jnp.arange(N, dtype=jnp.int32)
    phase = row_index[..., None] * columns % N
    angle = phase.astype(jnp.float32) * (2.0 * math.pi / N)
    scale = 1.0 / math.sqrt(N)
    return ((jnp.cos(angle) * scale).astype(jnp.bfloat16), (-jnp.sin(angle) * scale).astype(jnp.bfloat16))

def facet_mask(width):
    offsets = jnp.arange(E, dtype=jnp.int32)
    outside = jnp.maximum(jnp.maximum(HALO - offsets, offsets - (HALO + FS - 1)), 0)
    keep = (outside <= width).astype(jnp.float32)
    return (keep[:, None] * keep[None, :]).astype(jnp.bfloat16)

def kept_rows(rows_of_block):
    return (rows_of_block[:, None] * BLK + jnp.arange(BLK, dtype=jnp.int32)[None, :]).reshape(R * BLK).astype(jnp.int32)

def widen(values):
    return lax.optimization_barrier(values).astype(jnp.float32)

def shrink_block(block):
    channels = block.shape[0]
    block_half = block.astype(jnp.bfloat16)
    gram_matrix = jnp.dot(block_half.astype(jnp.float32), block_half.T.astype(jnp.float32), preferred_element_type=jnp.float32)
    ridge_level = shrink_ratio * (jnp.trace(gram_matrix) / channels + tiny_value)
    factor_lower = jnp.linalg.cholesky(gram_matrix + ridge_level * jnp.eye(channels, dtype=gram_matrix.dtype))
    return ridge_level * jax.scipy.linalg.cho_solve((factor_lower, True), block)

def reference(image, lowrank_dual, wavelet_dual, data_dual, observed, kernel_weights, analysis_matrix, block_rows, intersection_widths, ball_radii):
    channels = image.shape[0]
    zero_index = jnp.zeros((), jnp.int32)
    full_real, full_imag = dft_rows(jnp.arange(N, dtype=jnp.int32))
    weight_float = kernel_weights.astype(jnp.float32)
    matrix_float = analysis_matrix.astype(jnp.float32)
    weighted_dual = (data_dual * weight_float[None]).astype(jnp.bfloat16)

    def adjoint_channel(operands):
        weighted_channel, rows_channel = operands

        def adjoint_block(block_index):
            kept_real, kept_imag = dft_rows(kept_rows(rows_channel[block_index]))
            start = (block_index * BLK).astype(jnp.int32)
            part_real = lax.dynamic_slice_in_dim(weighted_channel[0], start, BLK, 1)
            part_imag = lax.dynamic_slice_in_dim(weighted_channel[1], start, BLK, 1)
            out_real = jnp.dot(kept_real.T.astype(jnp.float32), part_real.astype(jnp.float32), preferred_element_type=jnp.float32) + jnp.dot(kept_imag.T.astype(jnp.float32), part_imag.astype(jnp.float32), preferred_element_type=jnp.float32)
            out_imag = jnp.dot(kept_real.T.astype(jnp.float32), part_imag.astype(jnp.float32), preferred_element_type=jnp.float32) - jnp.dot(kept_imag.T.astype(jnp.float32), part_real.astype(jnp.float32), preferred_element_type=jnp.float32)
            return jnp.stack([out_real, out_imag]).astype(jnp.bfloat16)
        spread = lax.map(adjoint_block, jnp.arange(NB, dtype=jnp.int32))
        spread = spread.transpose(1, 2, 0, 3).reshape(2, N, N)
        back_image = jnp.dot(spread[0].astype(jnp.float32), full_real.astype(jnp.float32), preferred_element_type=jnp.float32) + jnp.dot(spread[1].astype(jnp.float32), full_imag.astype(jnp.float32), preferred_element_type=jnp.float32)
        return back_image.astype(jnp.bfloat16)
    adjoint_image = lax.map(adjoint_channel, (weighted_dual.transpose(1, 0, 2, 3), block_rows))

    def add_facet(facet_index, canvas):
        row_facet = (facet_index // FACETS).astype(jnp.int32)
        col_facet = (facet_index % FACETS).astype(jnp.int32)
        block = lax.dynamic_slice(wavelet_dual, (zero_index, row_facet * E, col_facet * E), (channels, E, E))
        half_done = jnp.einsum('ji,cjk->cik', matrix_float, widen(block.astype(jnp.bfloat16))).astype(jnp.bfloat16)
        mask_float = facet_mask(intersection_widths[row_facet, col_facet]).astype(jnp.float32)
        synthesized = jnp.einsum('cik,kl->cil', widen(half_done), matrix_float) * mask_float
        start = (zero_index, row_facet * FS, col_facet * FS)
        current = lax.dynamic_slice(canvas, start, (channels, E, E))
        return lax.dynamic_update_slice(canvas, current + synthesized, start)
    canvas = jnp.zeros((channels, N + 2 * HALO, N + 2 * HALO), jnp.float32)
    canvas = lax.fori_loop(0, FACETS * FACETS, add_facet, canvas)
    prior_synthesis = canvas[:, HALO:HALO + N, HALO:HALO + N]
    gradient = adjoint_image.astype(jnp.float32) + prior_synthesis + lowrank_dual
    image_next = jnp.maximum(image - step_size * gradient, 0.0)
    tilde = 2.0 * image_next - image
    tilde_half = tilde.astype(jnp.bfloat16)
    tilde_padded = jnp.pad(tilde_half, ((0, 0), (HALO, HALO), (HALO, HALO)))

    def analyse_facet(facet_index):
        row_facet = (facet_index // FACETS).astype(jnp.int32)
        col_facet = (facet_index % FACETS).astype(jnp.int32)
        piece = lax.dynamic_slice(tilde_padded, (zero_index, row_facet * FS, col_facet * FS), (channels, E, E))
        masked = piece * facet_mask(intersection_widths[row_facet, col_facet])
        half_coeffs = jnp.einsum('ij,cjk->cik', matrix_float, widen(masked)).astype(jnp.bfloat16)
        coefficients = jnp.einsum('cik,lk->cil', widen(half_coeffs), matrix_float)
        previous = lax.dynamic_slice(wavelet_dual, (zero_index, row_facet * E, col_facet * E), (channels, E, E))
        return jnp.clip(previous + coefficients, -clip_bound, clip_bound)
    stacked = lax.map(analyse_facet, jnp.arange(FACETS * FACETS, dtype=jnp.int32))
    wavelet_next = stacked.reshape(FACETS, FACETS, channels, E, E).transpose(2, 0, 3, 1, 4).reshape(channels, FACETS * E, FACETS * E)
    shifted_total = (lowrank_dual + tilde).reshape(channels, FACETS, FS, FACETS, FS).transpose(1, 3, 0, 2, 4).reshape(FACETS * FACETS, channels, FS * FS)
    lowrank_facets = lax.map(shrink_block, shifted_total)
    lowrank_next = lowrank_facets.reshape(FACETS, FACETS, channels, FS, FS).transpose(2, 0, 3, 1, 4).reshape(channels, N, N)

    def forward_channel(operands):
        tilde_channel, rows_channel = operands
        spec_real = jnp.dot(tilde_channel.astype(jnp.float32), full_real.astype(jnp.float32), preferred_element_type=jnp.float32).astype(jnp.bfloat16)
        spec_imag = jnp.dot(tilde_channel.astype(jnp.float32), full_imag.astype(jnp.float32), preferred_element_type=jnp.float32).astype(jnp.bfloat16)

        def forward_block(block_index):
            kept_real, kept_imag = dft_rows(kept_rows(rows_channel[block_index]))
            start = (block_index * BLK).astype(jnp.int32)
            part_real = lax.dynamic_slice_in_dim(spec_real, start, BLK, 1)
            part_imag = lax.dynamic_slice_in_dim(spec_imag, start, BLK, 1)
            out_real = jnp.dot(kept_real.astype(jnp.float32), part_real.astype(jnp.float32), preferred_element_type=jnp.float32) - jnp.dot(kept_imag.astype(jnp.float32), part_imag.astype(jnp.float32), preferred_element_type=jnp.float32)
            out_imag = jnp.dot(kept_real.astype(jnp.float32), part_imag.astype(jnp.float32), preferred_element_type=jnp.float32) + jnp.dot(kept_imag.astype(jnp.float32), part_real.astype(jnp.float32), preferred_element_type=jnp.float32)
            return jnp.stack([out_real, out_imag])
        blocks = lax.map(forward_block, jnp.arange(NB, dtype=jnp.int32))
        return blocks.transpose(1, 2, 0, 3).reshape(2, R * BLK, N)
    predicted = lax.map(forward_channel, (tilde_half, block_rows)).transpose(1, 0, 2, 3)
    residual = data_dual + weight_float[None] * predicted - observed
    block_shape = (2, channels, R * BLK, NB, BLK)
    blocks_residual = residual.reshape(block_shape)
    block_norm = jnp.sqrt(lax.optimization_barrier(jnp.sum(blocks_residual * blocks_residual, axis=(0, 2, 4))))
    shrink_factor = jnp.maximum(0.0, 1.0 - ball_radii / jnp.maximum(block_norm, ball_radii))
    data_next = (blocks_residual * shrink_factor[None, :, None, :, None]).reshape(2, channels, R * BLK, N)
    return (image_next, lowrank_next, wavelet_next, data_next)
```

```python
from functools import partial
import math

import jax
import jax.numpy as jnp
import ml_dtypes
import numpy as np
from jax import lax
from jax.sharding import PartitionSpec as P

N = 2048
FS = 128
HALO = 64
E = 256
BLK = 128
R = 4


step_size = 0.5
clip_bound = 1.5
shrink_ratio = 0.5
tiny_value = 1e-06


def padded_2(x, sides, width):
    for axis, dim in sides:
        size, length = (lax.axis_size(axis), x.shape[dim])
        up = [(i, (i + 1) % size) for i in range(size - 1)]
        down = [(j, i) for i, j in up]
        last = lax.slice_in_dim(x, length - width, length, axis=dim)
        first = lax.slice_in_dim(x, 0, width, axis=dim)
        before = lax.ppermute(last, axis, up)
        after = lax.ppermute(first, axis, down)
        x = jnp.concatenate([before, x, after], axis=dim)
    return x


def dft_table():
    index = np.arange(N, dtype=np.int64)
    angle = (index[:, None] * index[None, :] % N) * (2.0 * math.pi / N)
    scale = 1.0 / math.sqrt(N)
    return np.stack([np.cos(angle) * scale, -np.sin(angle) * scale]).astype(ml_dtypes.bfloat16)


def facet_mask(width):
    offsets = jnp.arange(E, dtype=jnp.int32)
    outside = jnp.maximum(jnp.maximum(HALO - offsets, offsets - (HALO + FS - 1)), 0)
    keep = (outside <= width).astype(jnp.float32)
    return (keep[:, None] * keep[None, :]).astype(jnp.bfloat16)


def shrink_block(block):
    channels = block.shape[0]
    block_half = block.astype(jnp.bfloat16)
    gram_matrix = jnp.dot(block_half, block_half.T, preferred_element_type=jnp.float32)
    ridge_level = shrink_ratio * (jnp.trace(gram_matrix) / channels + tiny_value)
    factor_lower = jnp.linalg.cholesky(
        gram_matrix + ridge_level * jnp.eye(channels, dtype=gram_matrix.dtype)
    )
    return ridge_level * jax.scipy.linalg.cho_solve((factor_lower, True), block)


def fold_margin(values, along_dim, inner_size):
    upper = lax.slice_in_dim(values, 0, HALO, axis=along_dim)
    lower = lax.slice_in_dim(values, inner_size + 3 * HALO, inner_size + 4 * HALO, axis=along_dim)
    middle = lax.slice_in_dim(values, 2 * HALO, 2 * HALO + inner_size, axis=along_dim)
    upper_pad = [(0, 0)] * values.ndim
    lower_pad = [(0, 0)] * values.ndim
    upper_pad[along_dim] = (0, inner_size - HALO)
    lower_pad[along_dim] = (inner_size - HALO, 0)
    return middle + jnp.pad(upper, upper_pad) + jnp.pad(lower, lower_pad)


def shards(
    image,
    lowrank_dual,
    wavelet_dual,
    data_dual,
    observed,
    kernel_weights,
    analysis_matrix,
    block_rows,
    intersection_widths,
    ball_radii,
):
    channels, tile_rows, tile_cols = image.shape
    group_size = block_rows.shape[0]
    local_blocks = block_rows.shape[1]
    local_columns = data_dual.shape[3]
    facet_rows = tile_rows // FS
    facet_cols = tile_cols // FS
    facet_count = facet_rows * facet_cols
    product = partial(jnp.einsum, preferred_element_type=jnp.float32)
    full_table = jnp.asarray(dft_table())
    kept_real, kept_imag = (
        jnp.take(part.reshape(N // BLK, BLK, N), block_rows, axis=0).reshape(
            group_size, local_blocks, R * BLK, N
        )
        for part in full_table
    )
    weight_float = kernel_weights.astype(jnp.float32).reshape(
        group_size, R * BLK, local_blocks, BLK
    )[None]
    block_shape = (2, group_size, R * BLK, local_blocks, BLK)
    weighted_dual = (data_dual.reshape(block_shape) * weight_float).astype(jnp.bfloat16)
    adjoint_real = product("gjkr,gkjb->grjb", kept_real, weighted_dual[0]) + product(
        "gjkr,gkjb->grjb", kept_imag, weighted_dual[1]
    )
    adjoint_imag = product("gjkr,gkjb->grjb", kept_real, weighted_dual[1]) - product(
        "gjkr,gkjb->grjb", kept_imag, weighted_dual[0]
    )
    spread = (
        jnp.stack([adjoint_real, adjoint_imag])
        .astype(jnp.bfloat16)
        .reshape(2, group_size, N, local_columns)
    )
    rows_back = lax.all_to_all(spread, "facet", split_axis=2, concat_axis=3, tiled=True)
    back_image = product("pgrv,pvk->grk", rows_back, full_table).astype(jnp.bfloat16)
    adjoint_image = lax.all_to_all(back_image, "chan", split_axis=2, concat_axis=0, tiled=True)
    positions = [
        (row_slot, col_slot) for row_slot in range(facet_rows) for col_slot in range(facet_cols)
    ]
    facet_masks = jnp.stack(
        [facet_mask(intersection_widths[row_slot, col_slot]) for row_slot, col_slot in positions]
    )
    coeff_facets = (
        wavelet_dual.reshape(channels, facet_rows, E, facet_cols, E)
        .transpose(1, 3, 0, 2, 4)
        .reshape(facet_count, channels, E, E)
    )
    half_done = product("ji,fcjk->fcik", analysis_matrix, coeff_facets.astype(jnp.bfloat16)).astype(
        jnp.bfloat16
    )
    synthesized = (
        product("fcik,kl->fcil", half_done, analysis_matrix)
        * facet_masks.astype(jnp.float32)[:, None]
    )
    canvas = jnp.zeros((channels, tile_rows + 2 * HALO, tile_cols + 2 * HALO), jnp.float32)
    for position, (row_slot, col_slot) in enumerate(positions):
        canvas = canvas.at[
            :, row_slot * FS : row_slot * FS + E, col_slot * FS : col_slot * FS + E
        ].add(synthesized[position])
    received = padded_2(canvas, (("chan", 2), ("facet", 1)), HALO)
    folded = fold_margin(received, 1, tile_rows)
    prior_synthesis = fold_margin(folded, 2, tile_cols)
    gradient = adjoint_image.astype(jnp.float32) + prior_synthesis + lowrank_dual
    image_next = jnp.maximum(image - step_size * gradient, 0.0)
    tilde = 2.0 * image_next - image
    tilde_half = tilde.astype(jnp.bfloat16)
    padded = padded_2(tilde_half, (("chan", 2), ("facet", 1)), HALO)
    pieces = (
        jnp.stack(
            [
                padded[:, row_slot * FS : row_slot * FS + E, col_slot * FS : col_slot * FS + E]
                for row_slot, col_slot in positions
            ]
        )
        * facet_masks[:, None]
    )
    half_coeffs = product("ij,fcjk->fcik", analysis_matrix, pieces).astype(jnp.bfloat16)
    coefficients = product("fcik,lk->fcil", half_coeffs, analysis_matrix)
    wavelet_next = jnp.clip(coeff_facets + coefficients, -clip_bound, clip_bound)
    wavelet_next = (
        wavelet_next.reshape(facet_rows, facet_cols, channels, E, E)
        .transpose(2, 0, 3, 1, 4)
        .reshape(channels, facet_rows * E, facet_cols * E)
    )
    shifted_total = (
        (lowrank_dual + tilde)
        .reshape(channels, facet_rows, FS, facet_cols, FS)
        .transpose(1, 3, 0, 2, 4)
        .reshape(facet_count, channels, FS * FS)
    )
    lowrank_facets = jax.vmap(shrink_block)(shifted_total)
    lowrank_next = (
        lowrank_facets.reshape(facet_rows, facet_cols, channels, FS, FS)
        .transpose(2, 0, 3, 1, 4)
        .reshape(channels, tile_rows, tile_cols)
    )
    regrouped = lax.all_to_all(tilde_half, "chan", split_axis=0, concat_axis=2, tiled=True)
    spectrum = product("grk,pkv->pgrv", regrouped, full_table).astype(jnp.bfloat16)
    spectra_cols = lax.all_to_all(
        spectrum, "facet", split_axis=3, concat_axis=2, tiled=True
    ).reshape(2, group_size, N, local_blocks, BLK)
    forward_real = product("gjkr,grjb->gkjb", kept_real, spectra_cols[0]) - product(
        "gjkr,grjb->gkjb", kept_imag, spectra_cols[1]
    )
    forward_imag = product("gjkr,grjb->gkjb", kept_real, spectra_cols[1]) + product(
        "gjkr,grjb->gkjb", kept_imag, spectra_cols[0]
    )
    predicted = jnp.stack([forward_real, forward_imag])
    residual = (
        data_dual.reshape(block_shape) + weight_float * predicted - observed.reshape(block_shape)
    )
    block_norm = jnp.sqrt(jnp.sum(residual * residual, axis=(0, 2, 4)))
    shrink_factor = jnp.maximum(0.0, 1.0 - ball_radii / jnp.maximum(block_norm, ball_radii))
    data_next = (residual * shrink_factor[None, :, None, :, None]).reshape(
        2, group_size, R * BLK, local_columns
    )
    return (image_next, lowrank_next, wavelet_next, data_next)


def solution(mesh):
    in_specs = (
        P(None, "facet", "chan"),
        P(None, "facet", "chan"),
        P(None, "facet", "chan"),
        P(None, "chan", None, "facet"),
        P(None, "chan", None, "facet"),
        P("chan", None, "facet"),
        P(),
        P("chan", "facet", None),
        P("facet", "chan"),
        P("chan", "facet"),
    )
    out_specs = (
        P(None, "facet", "chan"),
        P(None, "facet", "chan"),
        P(None, "facet", "chan"),
        P(None, "chan", None, "facet"),
    )
    return jax.shard_map(shards, mesh=mesh, in_specs=in_specs, out_specs=out_specs, check_vma=False)
```

```python
import math
from functools import partial

import jax
import jax.numpy as jnp
import ml_dtypes
import numpy as np
from jax import lax
from jax.experimental import pallas as pl
from jax.experimental.pallas import tpu as pltpu
from jax.sharding import PartitionSpec as P

N = 2048
FS = 128
HALO = 64
E = 256
BLK = 128
R = 4
C = 8
NB = 16
CHUNKS = 4
ROWS = N // CHUNKS

step_size = 0.5
clip_bound = 1.5
shrink_ratio = 0.5
tiny_value = 1e-06

MESH = pl.DeviceIdType.MESH
f32 = jnp.float32
bf16 = jnp.bfloat16


def dft_table():
    index = np.arange(N, dtype=np.int64)
    angle = (index[:, None] * index[None, :] % N) * (2.0 * math.pi / N)
    scale = 1.0 / math.sqrt(N)
    parts = np.stack([np.cos(angle) * scale, -np.sin(angle) * scale])
    return (
        parts.reshape(2, N, NB, BLK)
        .transpose(1, 2, 0, 3)
        .reshape(N, 2 * N)
        .astype(ml_dtypes.bfloat16)
    )


def dot(a, b):
    return lax.dot_general(a, b, (((1,), (0,)), ((), ())), preferred_element_type=f32)


def dot_nt(a, b):
    return lax.dot_general(a, b, (((1,), (1,)), ((), ())), preferred_element_type=f32)


def swap_halves(x):
    return pltpu.roll(x, HALO, 1)


def lane_low(shape):
    return lax.broadcasted_iota(jnp.int32, shape, 1) < HALO


def facet_masks(width, up, down, left, right):
    row = lax.broadcasted_iota(jnp.int32, (E, FS), 0)
    away = jnp.maximum(jnp.maximum(HALO - row, row - (HALO + FS - 1)), 0)
    rows_in = (away <= width) & ((row >= HALO) | up) & ((row < HALO + FS) | down)
    lane = lax.broadcasted_iota(jnp.int32, (E, FS), 1)
    low = lane < HALO
    away = jnp.where(low, lane + 1, FS - lane)
    lanes_in = (away <= width) & ((low & right) | (jnp.logical_not(low) & left))
    return rows_in, rows_in & lanes_in


def body(
    rows_ref,
    widths_ref,
    radii_ref,
    matrix_ref,
    image_hbm,
    lowrank_hbm,
    wavelet_hbm,
    dual_hbm,
    observed_hbm,
    weights_hbm,
    table_hbm,
    image_out,
    lowrank_out,
    wavelet_out,
    data_out,
    t0,
    t1,
    t2,
    t3,
    first_columns,
    first_rows,
    phases,
    wav,
    img,
    low,
    dual,
    obs,
    wgt,
    weighted,
    spread,
    rows_back,
    acc,
    adj_send,
    adj_recv,
    turned,
    rolled,
    syn,
    syn_left,
    syn_right,
    center,
    from_up,
    from_down,
    from_left,
    from_left_corner,
    from_right,
    from_right_corner,
    padded,
    edge_left,
    edge_right,
    halo_left,
    halo_right,
    regrouped,
    spec,
    spec_recv,
    forward,
    gram,
    shrink,
    low_next,
    table_sem,
    wav_sem,
    in_sem,
    out_sem,
    wav_out_sem,
    low_out_sem,
    a1s,
    a1r,
    a2s,
    a2r,
    a3s,
    a3r,
    a4s,
    a4r,
    h1s,
    h1r,
    h2s,
    h2r,
):
    tables = (t0, t1, t2, t3)
    c = lax.axis_index("chan")
    p = lax.axis_index("facet")
    up, down = lax.rem(p + NB - 1, NB), lax.rem(p + 1, NB)
    left, right = lax.rem(c + C - 1, C), lax.rem(c + 1, C)
    group = p // (NB // CHUNKS)
    held = [lax.rem(group + t, CHUNKS) for t in range(CHUNKS)]

    small = [
        pltpu.make_async_copy(src, dst, in_sem.at[k])
        for k, (src, dst) in enumerate(
            (
                (dual_hbm, dual),
                (weights_hbm, wgt),
                (image_hbm, img),
                (lowrank_hbm, low),
                (observed_hbm, obs),
            )
        )
    ]
    small[0].start()
    small[1].start()
    column_copy = pltpu.make_async_copy(
        table_hbm.at[pl.ds(0, N), pl.ds(0, E)], first_columns, in_sem.at[5]
    )
    column_copy.start()
    row_copy = pltpu.make_async_copy(table_hbm.at[pl.ds(0, BLK)], first_rows, in_sem.at[6])
    table_copies = []
    for t in range(CHUNKS):
        start = pl.multiple_of(held[t] * ROWS, ROWS)
        copy = pltpu.make_async_copy(table_hbm.at[pl.ds(start, ROWS)], tables[t], table_sem.at[t])
        copy.start()
        table_copies.append(copy)
    for k in range(C):
        pltpu.make_async_copy(wavelet_hbm.at[k], wav.at[k], wav_sem.at[k]).start()
    for k in range(2, 5):
        small[k].start()
    row_copy.start()

    barrier = pltpu.get_barrier_semaphore()

    def greet_facet(s, carry):
        peer = lax.rem(p + s, NB)
        pl.semaphore_signal(barrier, inc=1, device_id=(c, peer), device_id_type=MESH)
        return carry

    def greet_chan(s, carry):
        peer = lax.rem(c + s, C)
        pl.semaphore_signal(barrier, inc=1, device_id=(peer, p), device_id_type=MESH)
        return carry

    lax.fori_loop(1, NB, greet_facet, 0)
    lax.fori_loop(1, C, greet_chan, 0)
    for a in (left, right):
        for b in (up, down):
            pl.semaphore_signal(barrier, inc=1, device_id=(a, b), device_id_type=MESH)

    matrix = matrix_ref[...]
    turned[...] = matrix.astype(f32).T.astype(bf16)
    rolled[...] = pltpu.roll(matrix.astype(f32), E - HALO, 1).astype(bf16)

    row16 = lax.broadcasted_iota(jnp.int32, (NB, BLK), 0)
    for q in range(R):
        turn = (rows_ref[0, 0, q] * row16) & (NB - 1)
        cosine, sine = jnp.zeros((NB, BLK), f32), jnp.zeros((NB, BLK), f32)
        for m in range(NB):
            cosine = jnp.where(turn == m, math.cos(2.0 * math.pi * m / NB), cosine)
            sine = jnp.where(turn == m, math.sin(2.0 * math.pi * m / NB), sine)
        phases[q, 0] = cosine
        phases[q, 1] = sine

    small[0].wait()
    small[1].wait()
    for q in range(R):
        span = slice(q * BLK, (q + 1) * BLK)
        weight = wgt[span, :].astype(f32)
        real = (dual[0, span, :] * weight).astype(bf16)
        imag = (dual[1, span, :] * weight).astype(bf16)
        lanes_real = slice(q * E, q * E + BLK)
        lanes_imag = slice(q * E + BLK, (q + 1) * E)
        weighted[:BLK, lanes_real] = real
        weighted[:BLK, lanes_imag] = imag
        weighted[BLK:, lanes_real] = imag
        weighted[BLK:, lanes_imag] = -real

    def remote(src, dst, send, recv, chan, facet):
        return pltpu.make_async_remote_copy(
            src_ref=src,
            dst_ref=dst,
            send_sem=send,
            recv_sem=recv,
            device_id=(chan, facet),
            device_id_type=MESH,
        )

    column_copy.wait()
    pl.semaphore_wait(barrier, NB - 1 + C - 1 + 4)

    def spread_pair(s, carry):
        pair = lax.rem(p // 2 + s, NB // 2)
        start = pl.multiple_of(pair * 2 * FS, 2 * FS)
        out = dot(first_columns[pl.ds(start, 2 * FS), :], weighted[...])
        real, imag = None, None
        for q in range(R):
            part_real = out[:, q * E : q * E + BLK].reshape(16, NB, BLK)
            part_imag = out[:, q * E + BLK : (q + 1) * E].reshape(16, NB, BLK)
            cosine, sine = phases[q, 0][None], phases[q, 1][None]
            term_real = cosine * part_real - sine * part_imag
            term_imag = cosine * part_imag + sine * part_real
            real = term_real if real is None else real + term_real
            imag = term_imag if imag is None else imag + term_imag
        rounded = jnp.concatenate(
            [real.reshape(2 * FS, BLK), imag.reshape(2 * FS, BLK)], axis=1
        ).astype(bf16)
        for k in range(2):
            target = pair * 2 + k
            block = rounded[k * FS : (k + 1) * FS]
            spread[target] = block

            @pl.when(target != p)
            def _():
                remote(
                    spread.at[target], rows_back.at[p], a1s.at[target], a1r.at[p], c, target
                ).start()

            @pl.when(target == p)
            def _():
                rows_back[p] = block

        return carry

    lax.fori_loop(1, NB // 2 + 1, spread_pair, 0)

    is_low = lane_low((E, FS))
    valid_up, valid_down = p > 0, p < NB - 1
    valid_left, valid_right = c > 0, c < C - 1

    def synth_channel(k, masks):
        pltpu.make_async_copy(wavelet_hbm.at[k], wav.at[k], wav_sem.at[k]).wait()
        half = dot(turned[...], wav[k].astype(bf16)).astype(bf16)
        cores, margins = [], []
        for f in range(2):
            out = dot(half[:, f * E : (f + 1) * E], rolled[...])
            rows_in, both = masks[f]
            cores.append(jnp.where(rows_in, out[:, :FS], 0.0))
            margins.append(jnp.where(both, out[:, FS:], 0.0))
        tile0 = cores[0] + jnp.where(is_low, 0.0, margins[1])
        tile1 = cores[1] + jnp.where(is_low, margins[0], 0.0)
        syn[k, :, :FS] = tile0.astype(bf16)
        syn[k, :, FS:] = tile1.astype(bf16)
        center[k, :, :FS] = tile0[HALO : HALO + FS]
        center[k, :, FS:] = tile1[HALO : HALO + FS]
        return margins

    true = p >= 0

    def synth_pair(k, carry):
        masks = [facet_masks(widths_ref[0, f], true, true, true, true) for f in range(2)]
        first = synth_channel(k, masks)
        second = synth_channel(k + 4, masks)
        syn_left[k] = jnp.where(is_low, swap_halves(second[0]), first[0]).astype(bf16)
        syn_right[k] = jnp.where(is_low, first[1], swap_halves(second[1])).astype(bf16)
        return carry

    lax.fori_loop(0, 4, synth_pair, 0)

    top, mid, bottom = pl.ds(0, HALO), pl.ds(HALO, FS), pl.ds(HALO + FS, HALO)
    first_half, second_half = pl.ds(0, HALO), pl.ds(HALO, HALO)
    every = slice(None)
    margin_copies = [
        remote(src, dst, h1s.at[k], h1r.at[k], a, b)
        for k, (src, dst, a, b) in enumerate(
            (
                (syn.at[every, top], from_down, c, up),
                (syn.at[every, bottom], from_up, c, down),
                (syn_left.at[every, mid], from_right, left, p),
                (syn_right.at[every, mid], from_left, right, p),
                (syn_left.at[every, top], from_right_corner.at[every, second_half], left, up),
                (syn_left.at[every, bottom], from_right_corner.at[every, first_half], left, down),
                (syn_right.at[every, top], from_left_corner.at[every, second_half], right, up),
                (syn_right.at[every, bottom], from_left_corner.at[every, first_half], right, down),
            )
        )
    ]
    for copy in margin_copies:
        copy.start()

    acc[...] = jnp.zeros_like(acc)
    for copy in table_copies:
        copy.wait()

    def back_block(s, carry):
        j = lax.rem(p + s, NB)

        @pl.when(s > 0)
        def _():
            remote(rows_back.at[j], rows_back.at[j], a1s.at[j], a1r.at[j], c, j).wait_recv()

        block = rows_back[j]
        start = pl.multiple_of(j * E, E)
        for t in range(CHUNKS):
            acc[t] += dot_nt(block, tables[t][:, pl.ds(start, E)])
        return carry

    lax.fori_loop(0, NB, back_block, 0)

    for t in range(CHUNKS):
        for k in range(2):
            target = held[t] * 2 + k
            adj_send[2 * t + k] = acc[t, :, k * E : (k + 1) * E].astype(bf16)

            @pl.when(target != c)
            def _():
                remote(
                    adj_send.at[2 * t + k], adj_recv.at[c], a2s.at[target], a2r.at[c], target, p
                ).start()

            @pl.when(target == c)
            def _():
                adj_recv[c] = adj_send[2 * t + k]

    small[2].wait()
    small[3].wait()
    small[4].wait()
    for copy in margin_copies:
        copy.wait_recv()
    half_low = lane_low((FS, FS))
    zero = jnp.zeros((), f32)

    def gather_prior(k, carry):
        pair = lax.rem(k, 4)
        is_first = k < 4
        row = lax.broadcasted_iota(jnp.int32, (FS, FS), 0)
        corner_ok = ((row < HALO) & valid_up) | ((row >= HALO) & valid_down)
        sides = from_left[pair].astype(f32) + jnp.where(
            corner_ok, from_left_corner[pair].astype(f32), 0.0
        )
        sides = jnp.where(is_first, sides, swap_halves(sides))
        tile0 = jnp.where(half_low & valid_left, sides, 0.0)
        sides = from_right[pair].astype(f32) + jnp.where(
            corner_ok, from_right_corner[pair].astype(f32), 0.0
        )
        sides = jnp.where(is_first, sides, swap_halves(sides))
        tile1 = jnp.where(jnp.logical_not(half_low) & valid_right, sides, 0.0)
        above = jnp.where(valid_up, from_up[k].astype(f32), 0.0)
        below = jnp.where(valid_down, from_down[k].astype(f32), 0.0)
        sides = jnp.concatenate([tile0, tile1], axis=1)
        vertical = jnp.concatenate([above, below], axis=0)
        prior = center[k] + sides + vertical
        center[k] = img[k] - step_size * (prior + low[k])
        return carry

    lax.fori_loop(0, C, gather_prior, 0)

    def image_step(s, carry):
        k = lax.rem(c + s, C)

        @pl.when(s > 0)
        def _():
            remote(adj_recv.at[k], adj_recv.at[k], a2s.at[k], a2r.at[k], k, p).wait_recv()

        updated = jnp.maximum(center[k] - step_size * adj_recv[k].astype(f32), 0.0)
        tilde = 2.0 * updated - img[k]
        center[k] = updated
        padded[k, HALO : HALO + FS, :] = tilde.astype(bf16)
        low[k] = low[k] + tilde

        @pl.when(s > 0)
        def _():
            remote(
                padded.at[k, mid], regrouped.at[c], a3s.at[k], a3r.at[c], k, p
            ).start()

        @pl.when(s == 0)
        def _():
            regrouped[c] = tilde.astype(bf16)

        return carry

    lax.fori_loop(0, C, image_step, 0)
    image_copy = pltpu.make_async_copy(center, image_out, out_sem.at[0])
    image_copy.start()

    def pack_edges(k, carry):
        first = padded[k, HALO : HALO + FS, :].astype(f32)
        second = padded[k + 4, HALO : HALO + FS, :].astype(f32)
        edge_right[k] = jnp.where(
            half_low, swap_halves(second[:, FS:]), first[:, FS:]
        ).astype(bf16)
        edge_left[k] = jnp.where(
            half_low, first[:, :FS], swap_halves(second[:, :FS])
        ).astype(bf16)
        return carry

    lax.fori_loop(0, 4, pack_edges, 0)
    upper, lower = pl.ds(HALO, HALO), pl.ds(FS, HALO)
    halo_copies = [
        remote(src, dst, h2s.at[k], h2r.at[k], a, b)
        for k, (src, dst, a, b) in enumerate(
            (
                (padded.at[every, upper], padded.at[every, bottom], c, up),
                (padded.at[every, lower], padded.at[every, top], c, down),
                (edge_left, halo_right.at[every, mid], left, p),
                (edge_right, halo_left.at[every, mid], right, p),
                (edge_left.at[every, first_half], halo_right.at[every, bottom], left, up),
                (edge_left.at[every, second_half], halo_right.at[every, top], left, down),
                (edge_right.at[every, first_half], halo_left.at[every, bottom], right, up),
                (edge_right.at[every, second_half], halo_left.at[every, top], right, down),
            )
        )
    ]
    for copy in halo_copies:
        copy.start()

    for f in range(2):
        lanes = slice(f * FS, (f + 1) * FS)

        def gram_row(a, carry):
            mine = low[a, :, lanes].astype(bf16).astype(f32)
            for b in range(C):
                other = low[b, :, lanes].astype(bf16).astype(f32)
                gram[a, b : b + 1, :] = jnp.sum(mine * other, axis=0, keepdims=True)
            return carry

        lax.fori_loop(0, C, gram_row, 0)
        total = jnp.sum(gram[...], axis=2)
        row = lax.broadcasted_iota(jnp.int32, (C, C), 0)
        col = lax.broadcasted_iota(jnp.int32, (C, C), 1)
        eye = (row == col).astype(f32)
        trace = jnp.sum(jnp.sum(total * eye, axis=1, keepdims=True), axis=0, keepdims=True)
        ridge = shrink_ratio * (trace / C + tiny_value)
        system = total + ridge * eye
        inverse = eye
        for k in range(C):
            pivot = 1.0 / system[k : k + 1, k : k + 1]
            row_s = system[k : k + 1, :] * pivot
            row_i = inverse[k : k + 1, :] * pivot
            column = jnp.where(row == k, 0.0, jnp.broadcast_to(system[:, k : k + 1], (C, C)))
            system = jnp.where(row == k, jnp.broadcast_to(row_s, (C, C)), system - column * row_s)
            inverse = jnp.where(row == k, jnp.broadcast_to(row_i, (C, C)), inverse - column * row_i)
        inverse = ridge * inverse
        for k in range(C):
            shrink[k] = jnp.broadcast_to(inverse[:, k : k + 1], (C, FS))

        def apply_row(r, carry):
            span = pl.ds(pl.multiple_of(r * 16, 16), 16)
            blocks = [low[b, span, lanes] for b in range(C)]
            for a in range(C):
                out = None
                for b in range(C):
                    term = shrink[b, a : a + 1, :] * blocks[b]
                    out = term if out is None else out + term
                low_next[a, span, lanes] = out
            return carry

        lax.fori_loop(0, FS // 16, apply_row, 0)
    low_copy = pltpu.make_async_copy(low_next, lowrank_out, low_out_sem.at[0])
    low_copy.start()

    def arrive(s, carry):
        k = lax.rem(c + s, C)
        remote(regrouped.at[k], regrouped.at[k], a3s.at[k], a3r.at[k], k, p).wait_recv()
        return carry

    lax.fori_loop(1, C, arrive, 0)

    def spectrum_block(s, carry):
        j = lax.rem(p + s, NB)
        start = pl.multiple_of(j * E, E)
        total = None
        for t in range(CHUNKS):
            for k in range(2):
                term = dot(regrouped[held[t] * 2 + k], tables[t][k * E : (k + 1) * E, pl.ds(start, E)])
                total = term if total is None else total + term
        spec[j] = total.astype(bf16)

        @pl.when(s < NB)
        def _():
            remote(spec.at[j], spec_recv.at[p], a4s.at[j], a4r.at[p], c, j).start()

        @pl.when(s == NB)
        def _():
            spec_recv[p] = total.astype(bf16)

        return carry

    lax.fori_loop(1, NB + 1, spectrum_block, 0)

    for copy in halo_copies:
        copy.wait_recv()

    def analysis(k, carry):
        pair = lax.rem(k, 4)
        is_first = k < 4
        tiles = padded[k].astype(f32)
        tile0, tile1 = tiles[:, :FS], tiles[:, FS:]
        side = halo_left[pair].astype(f32)
        beside_left = jnp.where(is_first, side, swap_halves(side))
        side = halo_right[pair].astype(f32)
        beside_right = jnp.where(is_first, side, swap_halves(side))
        margins = (
            jnp.where(is_low, tile1, beside_left),
            jnp.where(is_low, beside_right, tile0),
        )
        for f in range(2):
            rows_in, both = facet_masks(
                widths_ref[0, f],
                valid_up,
                valid_down,
                valid_left if f == 0 else true,
                valid_right if f == 1 else true,
            )
            core = jnp.where(rows_in, tile0 if f == 0 else tile1, 0.0)
            margin = jnp.where(both, margins[f], 0.0)
            piece = jnp.concatenate([core, margin], axis=1).astype(bf16)
            half = dot(matrix_ref[...], piece).astype(bf16)
            coefficients = dot_nt(half, rolled[...])
            lanes = slice(f * E, (f + 1) * E)
            wav[k, :, lanes] = jnp.clip(wav[k, :, lanes] + coefficients, -clip_bound, clip_bound)
        pltpu.make_async_copy(wav.at[k], wavelet_out.at[k], wav_out_sem.at[k]).start()
        return carry

    lax.fori_loop(0, C, analysis, 0)

    forward[...] = jnp.zeros_like(forward)
    row_copy.wait()

    def forward_block(s, carry):
        j = lax.rem(p + s, NB)

        @pl.when(s > 0)
        def _():
            remote(spec_recv.at[j], spec_recv.at[j], a4s.at[j], a4r.at[j], c, j).wait_recv()

        block = spec_recv[j].astype(f32)
        real = block[:, :BLK].reshape(FS // NB, NB, BLK)
        imag = block[:, BLK:].reshape(FS // NB, NB, BLK)
        start = pl.multiple_of(j * E, E)
        rows_table = first_rows[:, pl.ds(start, E)]
        for q in range(R):
            cosine, sine = phases[q, 0][None], phases[q, 1][None]
            turned_real = (cosine * real + sine * imag).reshape(FS, BLK)
            turned_imag = (cosine * imag - sine * real).reshape(FS, BLK)
            upper_rows = jnp.concatenate([turned_real, turned_imag], axis=1)
            lower_rows = jnp.concatenate([-turned_imag, turned_real], axis=1)
            both = jnp.concatenate([upper_rows, lower_rows], axis=0).astype(bf16)
            forward[q * BLK : (q + 1) * BLK, :] += dot(rows_table, both)
        return carry

    lax.fori_loop(0, NB, forward_block, 0)

    weight = wgt[...].astype(f32)
    squares = jnp.zeros((1, BLK), f32)
    for part in range(2):
        residual = dual[part] + weight * forward[:, part * BLK : (part + 1) * BLK] - obs[part]
        dual[part] = residual
        squares = squares + jnp.sum(residual * residual, axis=0, keepdims=True)
    norm = jnp.sqrt(jnp.sum(squares, axis=1, keepdims=True))
    radius = radii_ref[0, 0]
    factor = jnp.maximum(0.0, 1.0 - radius / jnp.maximum(norm, radius))
    for part in range(2):
        dual[part] = dual[part] * factor
    data_copy = pltpu.make_async_copy(dual, data_out, out_sem.at[1])
    data_copy.start()

    def end_facet(s, carry):
        j = lax.rem(p + s, NB)
        remote(spec.at[j], spec_recv.at[j], a1s.at[j], a1r.at[j], c, j).wait_send()
        remote(spec.at[j], spec_recv.at[j], a4s.at[j], a4r.at[j], c, j).wait_send()
        return carry

    def end_chan(s, carry):
        k = lax.rem(c + s, C)
        remote(adj_send.at[k], adj_recv.at[k], a2s.at[k], a2r.at[k], k, p).wait_send()
        remote(padded.at[k, mid], regrouped.at[k], a3s.at[k], a3r.at[k], k, p).wait_send()
        return carry

    lax.fori_loop(1, NB, end_facet, 0)
    lax.fori_loop(1, C, end_chan, 0)
    for copy in margin_copies + halo_copies:
        copy.wait_send()
    image_copy.wait()
    low_copy.wait()

    def end_wavelet(k, carry):
        pltpu.make_async_copy(wav.at[k], wavelet_out.at[k], wav_out_sem.at[k]).wait()
        return carry

    lax.fori_loop(0, C, end_wavelet, 0)
    data_copy.wait()


def shards(
    image,
    lowrank_dual,
    wavelet_dual,
    data_dual,
    observed,
    kernel_weights,
    analysis_matrix,
    block_rows,
    intersection_widths,
    ball_radii,
):
    rows = R * BLK
    vmem = pltpu.VMEM
    dma = pltpu.SemaphoreType.DMA
    scratch = (
        [vmem((ROWS, 2 * N), bf16)] * 4
        + [
            vmem((N, E), bf16),
            vmem((BLK, 2 * N), bf16),
            vmem((R, 2, NB, BLK), f32),
            vmem((C, E, 2 * E), f32),
            vmem((C, FS, E), f32),
            vmem((C, FS, E), f32),
            vmem((2, rows, BLK), f32),
            vmem((2, rows, BLK), f32),
            vmem((rows, BLK), bf16),
            vmem((E, R * E), bf16),
            vmem((NB, FS, E), bf16),
            vmem((NB, FS, E), bf16),
            vmem((CHUNKS, FS, ROWS), f32),
            vmem((C, FS, E), bf16),
            vmem((C, FS, E), bf16),
            vmem((E, E), bf16),
            vmem((E, E), bf16),
            vmem((C, E, E), bf16),
            vmem((4, E, FS), bf16),
            vmem((4, E, FS), bf16),
            vmem((C, FS, E), f32),
            vmem((C, HALO, E), bf16),
            vmem((C, HALO, E), bf16),
            vmem((4, FS, FS), bf16),
            vmem((4, FS, FS), bf16),
            vmem((4, FS, FS), bf16),
            vmem((4, FS, FS), bf16),
            vmem((C, E, E), bf16),
            vmem((4, FS, FS), bf16),
            vmem((4, FS, FS), bf16),
            vmem((4, E, FS), bf16),
            vmem((4, E, FS), bf16),
            vmem((C, FS, E), bf16),
            vmem((NB, FS, E), bf16),
            vmem((NB, FS, E), bf16),
            vmem((rows, E), f32),
            vmem((C, C, FS), f32),
            vmem((C, C, FS), f32),
            vmem((C, FS, E), f32),
        ]
        + [dma((n,)) for n in (4, 8, 7, 2, 8, 1, 16, 16, 8, 8, 8, 8, 16, 16, 8, 8, 8, 8)]
    )
    hbm = pl.BlockSpec(memory_space=pl.ANY)
    smem = pl.BlockSpec(memory_space=pltpu.SMEM)
    image_next, lowrank_next, wavelet_next, data_next = pl.pallas_call(
        body,
        out_shape=(
            jax.ShapeDtypeStruct((C, FS, E), f32),
            jax.ShapeDtypeStruct((C, FS, E), f32),
            jax.ShapeDtypeStruct((C, E, 2 * E), f32),
            jax.ShapeDtypeStruct((2, rows, BLK), f32),
        ),
        in_specs=[smem] * 3 + [pl.BlockSpec(memory_space=pltpu.VMEM)] + [hbm] * 7,
        out_specs=(hbm,) * 4,
        scratch_shapes=scratch,
        compiler_params=pltpu.CompilerParams(
            collective_id=0, has_side_effects=True, vmem_limit_bytes=60 * 1024 * 1024
        ),
    )(
        block_rows,
        intersection_widths,
        ball_radii,
        analysis_matrix,
        image,
        lowrank_dual,
        wavelet_dual,
        data_dual.reshape(2, rows, BLK),
        observed.reshape(2, rows, BLK),
        kernel_weights.reshape(rows, BLK),
        jnp.asarray(dft_table()),
    )
    return image_next, lowrank_next, wavelet_next, data_next.reshape(2, 1, rows, BLK)


def solution(mesh):
    in_specs = (
        P(None, "facet", "chan"),
        P(None, "facet", "chan"),
        P(None, "facet", "chan"),
        P(None, "chan", None, "facet"),
        P(None, "chan", None, "facet"),
        P("chan", None, "facet"),
        P(),
        P("chan", "facet", None),
        P("facet", "chan"),
        P("chan", "facet"),
    )
    out_specs = (
        P(None, "facet", "chan"),
        P(None, "facet", "chan"),
        P(None, "facet", "chan"),
        P(None, "chan", None, "facet"),
    )
    return jax.shard_map(shards, mesh=mesh, in_specs=in_specs, out_specs=out_specs, check_vma=False)
```

```python
import math
from functools import partial

import jax
import jax.numpy as jnp
import ml_dtypes
import numpy as np
from jax import lax
from jax.experimental import pallas as pl
from jax.experimental.pallas import tpu as pltpu
from jax.sharding import PartitionSpec as P

N = 2048
FS = 128
HALO = 64
E = 256
BLK = 128
R = 4
C = 8
NB = 16
CHUNKS = 4
ROWS = N // CHUNKS
HALVES = 2
GROUP = 4
HR = FS // HALVES

step_size = 0.5
clip_bound = 1.5
shrink_ratio = 0.5
tiny_value = 1e-06

MESH = pl.DeviceIdType.MESH
f32 = jnp.float32
bf16 = jnp.bfloat16


def dft_table():
    index = np.arange(N, dtype=np.int64)
    angle = (index[:, None] * index[None, :] % N) * (2.0 * math.pi / N)
    scale = 1.0 / math.sqrt(N)
    parts = np.stack([np.cos(angle) * scale, -np.sin(angle) * scale])
    return (
        parts.reshape(2, N, NB, BLK)
        .transpose(1, 2, 0, 3)
        .reshape(N, 2 * N)
        .astype(ml_dtypes.bfloat16)
    )


def turned_table():
    return np.ascontiguousarray(dft_table().T)


def first_row_table():
    index = np.arange(N, dtype=np.int64)
    angle = (np.arange(BLK, dtype=np.int64)[:, None] * index[None, :] % N) * (2.0 * math.pi / N)
    scale = 1.0 / math.sqrt(N)
    parts = np.stack([np.cos(angle) * scale, -np.sin(angle) * scale])
    return (
        parts.reshape(2, BLK, NB // HALVES, HALVES, HALVES, HR)
        .transpose(1, 2, 4, 0, 3, 5)
        .reshape(BLK, 2 * N)
        .astype(ml_dtypes.bfloat16)
    )


def dot(a, b):
    return lax.dot_general(a, b, (((1,), (0,)), ((), ())), preferred_element_type=f32)


def dot_nt(a, b):
    return lax.dot_general(a, b, (((1,), (1,)), ((), ())), preferred_element_type=f32)


def swap_halves(x):
    return pltpu.roll(x, HALO, 1)


def lane_low(shape):
    return lax.broadcasted_iota(jnp.int32, shape, 1) < HALO


def facet_masks(width, up, down, left, right):
    row = lax.broadcasted_iota(jnp.int32, (E, FS), 0)
    away = jnp.maximum(jnp.maximum(HALO - row, row - (HALO + FS - 1)), 0)
    rows_in = (away <= width) & ((row >= HALO) | up) & ((row < HALO + FS) | down)
    lane = lax.broadcasted_iota(jnp.int32, (E, FS), 1)
    low = lane < HALO
    away = jnp.where(low, lane + 1, FS - lane)
    lanes_in = (away <= width) & ((low & right) | (jnp.logical_not(low) & left))
    return rows_in, rows_in & lanes_in


def body(
    rows_ref,
    widths_ref,
    radii_ref,
    matrix_ref,
    image_hbm,
    lowrank_hbm,
    wavelet_hbm,
    dual_hbm,
    observed_hbm,
    weights_hbm,
    table_hbm,
    row_table_hbm,
    turned_hbm,
    image_out,
    lowrank_out,
    wavelet_out,
    data_out,
    t0,
    t1,
    t2,
    t3,
    turned_rows,
    first_columns,
    first_rows,
    phases,
    wav,
    img,
    low,
    dual,
    obs,
    wgt,
    weighted,
    spread,
    rows_back,
    acc,
    adj_send,
    adj_recv,
    turned,
    rolled,
    syn,
    syn_left,
    syn_right,
    center,
    from_up,
    from_down,
    from_up_left,
    from_up_right,
    from_down_left,
    from_down_right,
    fold_left,
    fold_right,
    from_left,
    from_right,
    padded,
    edge_left,
    edge_right,
    halo_left,
    halo_right,
    regrouped,
    spec,
    spec_recv,
    forward,
    gram,
    shrink,
    low_next,
    table_sem,
    turned_sem,
    wav_sem,
    in_sem,
    out_sem,
    wav_out_sem,
    low_out_sem,
    a1s,
    a1r,
    a2s,
    a2r,
    a3s,
    a3r,
    a4s,
    a4r,
    h1s,
    h1r,
    h2s,
    h2r,
):
    tables = (t0, t1, t2, t3)
    c = lax.axis_index("chan")
    p = lax.axis_index("facet")
    up, down = lax.rem(p + NB - 1, NB), lax.rem(p + 1, NB)
    left, right = lax.rem(c + C - 1, C), lax.rem(c + 1, C)

    small = [
        pltpu.make_async_copy(src, dst, in_sem.at[k])
        for k, (src, dst) in enumerate(
            (
                (dual_hbm, dual),
                (weights_hbm, wgt),
                (image_hbm, img),
                (lowrank_hbm, low),
                (observed_hbm, obs),
            )
        )
    ]
    small[0].start()
    small[1].start()
    column_copy = pltpu.make_async_copy(
        table_hbm.at[pl.ds(0, N), pl.ds(0, E)], first_columns, in_sem.at[5]
    )
    column_copy.start()
    row_copy = pltpu.make_async_copy(row_table_hbm, first_rows, in_sem.at[6])
    table_copies = []
    for t in range(CHUNKS):
        copy = pltpu.make_async_copy(
            table_hbm.at[pl.ds(t * ROWS, ROWS)], tables[t], table_sem.at[t]
        )
        table_copies.append(copy)
    turned_copies = []
    for t in range(NB // GROUP):
        start = lax.rem(p // GROUP + t, NB // GROUP) * GROUP * E
        span = pl.ds(pl.multiple_of(start, GROUP * E), GROUP * E)
        turned_copies.append(
            pltpu.make_async_copy(turned_hbm.at[span], turned_rows.at[span], turned_sem.at[t])
        )

    barrier = pltpu.get_barrier_semaphore()

    def greet_facet(s, carry):
        peer = lax.rem(p + s, NB)
        pl.semaphore_signal(barrier, inc=1, device_id=(c, peer), device_id_type=MESH)
        return carry

    def greet_chan(s, carry):
        peer = lax.rem(c + s, C)
        pl.semaphore_signal(barrier, inc=1, device_id=(peer, p), device_id_type=MESH)
        return carry

    lax.fori_loop(1, NB, greet_facet, 0)
    lax.fori_loop(1, C, greet_chan, 0)

    matrix = matrix_ref[...]
    turned[...] = matrix.astype(f32).T.astype(bf16)
    rolled[...] = pltpu.roll(matrix.astype(f32), E - HALO, 1).astype(bf16)

    row16 = lax.broadcasted_iota(jnp.int32, (NB, BLK), 0)
    for q in range(R):
        turn = (rows_ref[0, 0, q] * row16) & (NB - 1)
        cosine, sine = jnp.zeros((NB, BLK), f32), jnp.zeros((NB, BLK), f32)
        for m in range(NB):
            cosine = jnp.where(turn == m, math.cos(2.0 * math.pi * m / NB), cosine)
            sine = jnp.where(turn == m, math.sin(2.0 * math.pi * m / NB), sine)
        phases[q, 0] = cosine
        phases[q, 1] = sine

    small[0].wait()
    small[1].wait()
    for q in range(R):
        span = slice(q * BLK, (q + 1) * BLK)
        weight = wgt[span, :].astype(f32)
        real = (dual[0, span, :] * weight).astype(bf16)
        imag = (dual[1, span, :] * weight).astype(bf16)
        lanes_real = slice(q * E, q * E + BLK)
        lanes_imag = slice(q * E + BLK, (q + 1) * E)
        weighted[:BLK, lanes_real] = real
        weighted[:BLK, lanes_imag] = imag
        weighted[BLK:, lanes_real] = imag
        weighted[BLK:, lanes_imag] = -real

    def remote(src, dst, send, recv, chan, facet):
        return pltpu.make_async_remote_copy(
            src_ref=src,
            dst_ref=dst,
            send_sem=send,
            recv_sem=recv,
            device_id=(chan, facet),
            device_id_type=MESH,
        )

    column_copy.wait()
    for k in range(C):
        pltpu.make_async_copy(wavelet_hbm.at[k], wav.at[k], wav_sem.at[k]).start()
    for copy in turned_copies:
        copy.start()
    for k in range(2, 5):
        small[k].start()
    for copy in table_copies:
        copy.start()
    row_copy.start()
    pl.semaphore_wait(barrier, NB - 1 + C - 1)

    def send_rows(target, half):
        remote(
            spread.at[target, half],
            rows_back.at[p, half],
            a1s.at[target * HALVES + half],
            a1r.at[p * HALVES + half],
            c,
            target,
        ).start()

    def spread_pair(s, carry):
        pair = lax.rem(p // 2 + s, NB // 2)
        start = pl.multiple_of(pair * 2 * FS, 2 * FS)
        out = dot(first_columns[pl.ds(start, 2 * FS), :], weighted[...])
        real, imag = None, None
        for q in range(R):
            part_real = out[:, q * E : q * E + BLK].reshape(16, NB, BLK)
            part_imag = out[:, q * E + BLK : (q + 1) * E].reshape(16, NB, BLK)
            cosine, sine = phases[q, 0][None], phases[q, 1][None]
            term_real = cosine * part_real - sine * part_imag
            term_imag = cosine * part_imag + sine * part_real
            real = term_real if real is None else real + term_real
            imag = term_imag if imag is None else imag + term_imag
        rounded = jnp.concatenate(
            [real.reshape(2 * FS, BLK), imag.reshape(2 * FS, BLK)], axis=1
        ).astype(bf16)
        for k in range(2):
            target = pair * 2 + k
            for half in range(HALVES):
                start = k * FS + half * HR
                spread[target, half] = rounded[start : start + HR]

            @pl.when(target != p)
            def _():
                send_rows(target, 0)

            @pl.when(target == p)
            def _():
                rows_back[p] = spread[target]

        return carry

    lax.fori_loop(1, NB // 2 + 1, spread_pair, 0)
    for half in range(1, HALVES):

        def send_later(s, carry):
            send_rows(lax.rem(p + s, NB), half)
            return carry

        lax.fori_loop(1, NB, send_later, 0)

    is_low = lane_low((E, FS))
    valid_up, valid_down = p > 0, p < NB - 1
    valid_left, valid_right = c > 0, c < C - 1

    def synth_channel(k, masks):
        pltpu.make_async_copy(wavelet_hbm.at[k], wav.at[k], wav_sem.at[k]).wait()
        half = dot(turned[...], wav[k].astype(bf16)).astype(bf16)
        cores, margins = [], []
        for f in range(2):
            out = dot(half[:, f * E : (f + 1) * E], rolled[...])
            rows_in, both = masks[f]
            cores.append(jnp.where(rows_in, out[:, :FS], 0.0))
            margins.append(jnp.where(both, out[:, FS:], 0.0))
        tile0 = cores[0] + jnp.where(is_low, 0.0, margins[1])
        tile1 = cores[1] + jnp.where(is_low, margins[0], 0.0)
        syn[k, :, :FS] = tile0.astype(bf16)
        syn[k, :, FS:] = tile1.astype(bf16)
        center[k, :, :FS] = tile0[HALO : HALO + FS]
        center[k, :, FS:] = tile1[HALO : HALO + FS]
        return margins

    true = p >= 0

    def synth_pair(k, carry):
        masks = [facet_masks(widths_ref[0, f], true, true, true, true) for f in range(2)]
        first = synth_channel(k, masks)
        second = synth_channel(k + 4, masks)
        syn_left[k] = jnp.where(is_low, swap_halves(second[0]), first[0]).astype(bf16)
        syn_right[k] = jnp.where(is_low, first[1], swap_halves(second[1])).astype(bf16)
        return carry

    lax.fori_loop(0, 4, synth_pair, 0)

    top, mid, bottom = pl.ds(0, HALO), pl.ds(HALO, FS), pl.ds(HALO + FS, HALO)
    every = slice(None)
    margin_copies = [
        remote(src, dst, h1s.at[k], h1r.at[k], a, b)
        for k, (src, dst, a, b) in enumerate(
            (
                (syn_left.at[every, top], from_down_left, c, up),
                (syn_left.at[every, bottom], from_up_left, c, down),
                (syn_right.at[every, top], from_down_right, c, up),
                (syn_right.at[every, bottom], from_up_right, c, down),
                (syn.at[every, top], from_down, c, up),
                (syn.at[every, bottom], from_up, c, down),
                (fold_left, from_right, left, p),
                (fold_right, from_left, right, p),
            )
        )
    ]
    for copy in margin_copies[:6]:
        copy.start()

    for copy in turned_copies:
        copy.wait()

    def back_half(half):
        acc[...] = jnp.zeros_like(acc)

        def back_group(s, carry):
            g = lax.rem(p // GROUP + s, NB // GROUP)

            def arrive(k, carry):
                j = g * GROUP + k

                @pl.when(j != p)
                def _():
                    index = j * HALVES + half
                    block = rows_back.at[j, half]
                    remote(block, block, a1s.at[index], a1r.at[index], c, j).wait_recv()

                return carry

            lax.fori_loop(0, GROUP, arrive, 0)
            block = jnp.concatenate([rows_back[g * GROUP + k, half] for k in range(GROUP)], axis=1)
            start = pl.multiple_of(g * GROUP * E, GROUP * E)
            for t in range(CHUNKS):
                lanes = slice(t * ROWS, (t + 1) * ROWS)
                acc[t] += dot(block, turned_rows[pl.ds(start, GROUP * E), lanes])
            return carry

        lax.fori_loop(0, NB // GROUP, back_group, 0)
        for target in range(C):
            lanes = slice((target % 2) * E, (target % 2 + 1) * E)
            adj_send[half, target] = acc[target // 2, :, lanes].astype(bf16)

        def send_image(s, carry):
            target = lax.rem(c + s, C)
            remote(
                adj_send.at[half, target],
                adj_recv.at[half, c],
                a2s.at[half * C + target],
                a2r.at[half * C + c],
                target,
                p,
            ).start()
            return carry

        lax.fori_loop(1, C, send_image, 0)
        adj_recv[half, c] = adj_send[half, c]

    back_half(0)

    for copy in margin_copies[:4]:
        copy.wait_recv()
    row = lax.broadcasted_iota(jnp.int32, (FS, FS), 0)
    side_ok = ((row < HALO) & valid_up) | ((row >= HALO) & valid_down)

    def fold_edges(k, carry):
        for own, above, below, out in (
            (syn_left, from_up_left, from_down_left, fold_left),
            (syn_right, from_up_right, from_down_right, fold_right),
        ):
            beside = jnp.concatenate([above[k], below[k]], axis=0).astype(f32)
            total = own[k, HALO : HALO + FS].astype(f32) + jnp.where(side_ok, beside, 0.0)
            out[k] = total.astype(bf16)
        return carry

    lax.fori_loop(0, 4, fold_edges, 0)
    for copy in margin_copies[6:]:
        copy.start()

    for half in range(1, HALVES):
        back_half(half)

    small[2].wait()
    small[3].wait()
    small[4].wait()
    for copy in margin_copies[4:]:
        copy.wait_recv()
    half_low = lane_low((FS, FS))

    def gather_prior(k, carry):
        pair = lax.rem(k, 4)
        is_first = k < 4
        sides = from_left[pair].astype(f32)
        sides = jnp.where(is_first, sides, swap_halves(sides))
        tile0 = jnp.where(half_low & valid_left, sides, 0.0)
        sides = from_right[pair].astype(f32)
        sides = jnp.where(is_first, sides, swap_halves(sides))
        tile1 = jnp.where(jnp.logical_not(half_low) & valid_right, sides, 0.0)
        above = jnp.where(valid_up, from_up[k].astype(f32), 0.0)
        below = jnp.where(valid_down, from_down[k].astype(f32), 0.0)
        sides = jnp.concatenate([tile0, tile1], axis=1)
        vertical = jnp.concatenate([above, below], axis=0)
        prior = center[k] + sides + vertical
        center[k] = img[k] - step_size * (prior + low[k])
        return carry

    lax.fori_loop(0, C, gather_prior, 0)

    def image_half(half):
        inside = slice(half * HR, (half + 1) * HR)
        here = pl.ds(HALO + half * HR, HR)

        def image_step(s, carry):
            k = lax.rem(c + s, C)

            @pl.when(s > 0)
            def _():
                index = half * C + k
                block = adj_recv.at[half, k]
                remote(block, block, a2s.at[index], a2r.at[index], k, p).wait_recv()

            adjoint = adj_recv[half, k].astype(f32)
            updated = jnp.maximum(center[k, inside] - step_size * adjoint, 0.0)
            tilde = 2.0 * updated - img[k, inside]
            center[k, inside] = updated
            padded[k, here] = tilde.astype(bf16)
            low[k, inside] = low[k, inside] + tilde

            @pl.when(s > 0)
            def _():
                remote(
                    padded.at[k, here],
                    regrouped.at[half, c],
                    a3s.at[half * C + k],
                    a3r.at[half * C + c],
                    k,
                    p,
                ).start()

            @pl.when(s == 0)
            def _():
                regrouped[half, c] = tilde.astype(bf16)

            return carry

        lax.fori_loop(0, C, image_step, 0)

    for half in range(HALVES):
        image_half(half)
    image_copy = pltpu.make_async_copy(center, image_out, out_sem.at[0])
    image_copy.start()

    def pack_edges(k, carry):
        first = padded[k, HALO : HALO + FS, :].astype(f32)
        second = padded[k + 4, HALO : HALO + FS, :].astype(f32)
        edge_right[k] = jnp.where(
            half_low, swap_halves(second[:, FS:]), first[:, FS:]
        ).astype(bf16)
        edge_left[k] = jnp.where(
            half_low, first[:, :FS], swap_halves(second[:, :FS])
        ).astype(bf16)
        return carry

    lax.fori_loop(0, 4, pack_edges, 0)
    upper, lower = pl.ds(HALO, HALO), pl.ds(FS, HALO)
    halo_copies = [
        remote(src, dst, h2s.at[k], h2r.at[k], a, b)
        for k, (src, dst, a, b) in enumerate(
            (
                (edge_left, halo_right.at[every, mid], left, p),
                (edge_right, halo_left.at[every, mid], right, p),
                (padded.at[every, upper], padded.at[every, bottom], c, up),
                (padded.at[every, lower], padded.at[every, top], c, down),
                (halo_left.at[every, upper], halo_left.at[every, bottom], c, up),
                (halo_left.at[every, lower], halo_left.at[every, top], c, down),
                (halo_right.at[every, upper], halo_right.at[every, bottom], c, up),
                (halo_right.at[every, lower], halo_right.at[every, top], c, down),
            )
        )
    ]
    for copy in halo_copies[:4]:
        copy.start()

    def spectrum_half(half):
        def arrive(s, carry):
            k = lax.rem(c + s, C)
            index = half * C + k
            block = regrouped.at[half, k]
            remote(block, block, a3s.at[index], a3r.at[index], k, p).wait_recv()
            return carry

        lax.fori_loop(1, C, arrive, 0)

        def spectrum_block(s, carry):
            j = lax.rem(p + s, NB)
            start = pl.multiple_of(j * E, E)
            total = None
            for q in range(C):
                rows_in = slice((q % 2) * E, (q % 2 + 1) * E)
                term = dot(regrouped[half, q], tables[q // 2][rows_in, pl.ds(start, E)])
                total = term if total is None else total + term
            spec[half, j] = total.astype(bf16)

            @pl.when(s < NB)
            def _():
                remote(
                    spec.at[half, j],
                    spec_recv.at[half, p],
                    a4s.at[half * NB + j],
                    a4r.at[half * NB + p],
                    c,
                    j,
                ).start()

            @pl.when(s == NB)
            def _():
                spec_recv[half, p] = total.astype(bf16)

            return carry

        lax.fori_loop(1, NB + 1, spectrum_block, 0)

    for copy in table_copies:
        copy.wait()
    spectrum_half(0)
    for copy in halo_copies[:2]:
        copy.wait_recv()
    for copy in halo_copies[4:]:
        copy.start()
    for half in range(1, HALVES):
        spectrum_half(half)

    for f in range(2):
        lanes = slice(f * FS, (f + 1) * FS)

        def gram_row(a, carry):
            mine = low[a, :, lanes].astype(bf16).astype(f32)
            for b in range(C):
                other = low[b, :, lanes].astype(bf16).astype(f32)
                gram[a, b : b + 1, :] = jnp.sum(mine * other, axis=0, keepdims=True)
            return carry

        lax.fori_loop(0, C, gram_row, 0)
        total = jnp.sum(gram[...], axis=2)
        row = lax.broadcasted_iota(jnp.int32, (C, C), 0)
        col = lax.broadcasted_iota(jnp.int32, (C, C), 1)
        eye = (row == col).astype(f32)
        trace = jnp.sum(jnp.sum(total * eye, axis=1, keepdims=True), axis=0, keepdims=True)
        ridge = shrink_ratio * (trace / C + tiny_value)
        system = total + ridge * eye
        inverse = eye
        for k in range(C):
            pivot = 1.0 / system[k : k + 1, k : k + 1]
            row_s = system[k : k + 1, :] * pivot
            row_i = inverse[k : k + 1, :] * pivot
            column = jnp.where(row == k, 0.0, jnp.broadcast_to(system[:, k : k + 1], (C, C)))
            system = jnp.where(row == k, jnp.broadcast_to(row_s, (C, C)), system - column * row_s)
            inverse = jnp.where(row == k, jnp.broadcast_to(row_i, (C, C)), inverse - column * row_i)
        inverse = ridge * inverse
        for k in range(C):
            shrink[k] = jnp.broadcast_to(inverse[:, k : k + 1], (C, FS))

        def apply_row(r, carry):
            span = pl.ds(pl.multiple_of(r * 16, 16), 16)
            blocks = [low[b, span, lanes] for b in range(C)]
            for a in range(C):
                out = None
                for b in range(C):
                    term = shrink[b, a : a + 1, :] * blocks[b]
                    out = term if out is None else out + term
                low_next[a, span, lanes] = out
            return carry

        lax.fori_loop(0, FS // 16, apply_row, 0)
    low_copy = pltpu.make_async_copy(low_next, lowrank_out, low_out_sem.at[0])
    low_copy.start()

    for copy in halo_copies[2:]:
        copy.wait_recv()

    def analysis(k, carry):
        pair = lax.rem(k, 4)
        is_first = k < 4
        tiles = padded[k].astype(f32)
        tile0, tile1 = tiles[:, :FS], tiles[:, FS:]
        side = halo_left[pair].astype(f32)
        beside_left = jnp.where(is_first, side, swap_halves(side))
        side = halo_right[pair].astype(f32)
        beside_right = jnp.where(is_first, side, swap_halves(side))
        margins = (
            jnp.where(is_low, tile1, beside_left),
            jnp.where(is_low, beside_right, tile0),
        )
        for f in range(2):
            rows_in, both = facet_masks(
                widths_ref[0, f],
                valid_up,
                valid_down,
                valid_left if f == 0 else true,
                valid_right if f == 1 else true,
            )
            core = jnp.where(rows_in, tile0 if f == 0 else tile1, 0.0)
            margin = jnp.where(both, margins[f], 0.0)
            piece = jnp.concatenate([core, margin], axis=1).astype(bf16)
            half = dot(matrix_ref[...], piece).astype(bf16)
            coefficients = dot_nt(half, rolled[...])
            lanes = slice(f * E, (f + 1) * E)
            wav[k, :, lanes] = jnp.clip(wav[k, :, lanes] + coefficients, -clip_bound, clip_bound)
        pltpu.make_async_copy(wav.at[k], wavelet_out.at[k], wav_out_sem.at[k]).start()
        return carry

    lax.fori_loop(0, C, analysis, 0)

    forward[...] = jnp.zeros_like(forward)
    row_copy.wait()

    def forward_block(s, carry):
        half = s // (NB // HALVES)
        g = lax.rem(p // HALVES + s, NB // HALVES)
        for b in range(HALVES):
            j = g * HALVES + b

            @pl.when(j != p)
            def _():
                index = half * NB + j
                block = spec_recv.at[half, j]
                remote(block, block, a4s.at[index], a4r.at[index], c, j).wait_recv()

        block = jnp.concatenate(
            [spec_recv[half, g * HALVES + b].astype(f32) for b in range(HALVES)], axis=0
        )
        real = block[:, :BLK].reshape(FS // NB, NB, BLK)
        imag = block[:, BLK:].reshape(FS // NB, NB, BLK)
        start = pl.multiple_of((g * HALVES + half) * E, E)
        rows_table = first_rows[:, pl.ds(start, E)]
        for q in range(R):
            cosine, sine = phases[q, 0][None], phases[q, 1][None]
            turned_real = (cosine * real + sine * imag).reshape(FS, BLK)
            turned_imag = (cosine * imag - sine * real).reshape(FS, BLK)
            upper_rows = jnp.concatenate([turned_real, turned_imag], axis=1)
            lower_rows = jnp.concatenate([-turned_imag, turned_real], axis=1)
            both = jnp.concatenate([upper_rows, lower_rows], axis=0).astype(bf16)
            forward[q * BLK : (q + 1) * BLK, :] += dot(rows_table, both)
        return carry

    lax.fori_loop(0, NB, forward_block, 0)

    weight = wgt[...].astype(f32)
    squares = jnp.zeros((1, BLK), f32)
    for part in range(2):
        residual = dual[part] + weight * forward[:, part * BLK : (part + 1) * BLK] - obs[part]
        dual[part] = residual
        squares = squares + jnp.sum(residual * residual, axis=0, keepdims=True)
    norm = jnp.sqrt(jnp.sum(squares, axis=1, keepdims=True))
    radius = radii_ref[0, 0]
    factor = jnp.maximum(0.0, 1.0 - radius / jnp.maximum(norm, radius))
    for part in range(2):
        dual[part] = dual[part] * factor
    data_copy = pltpu.make_async_copy(dual, data_out, out_sem.at[1])
    data_copy.start()

    def end_facet(s, carry):
        j = lax.rem(p + s, NB)
        for half in range(HALVES):
            block = spec_recv.at[half, j]
            sem = a1s.at[j * HALVES + half]
            remote(block, block, sem, a1r.at[0], c, j).wait_send()
            sem = a4s.at[half * NB + j]
            remote(block, block, sem, a4r.at[0], c, j).wait_send()
        return carry

    def end_chan(s, carry):
        k = lax.rem(c + s, C)
        for half in range(HALVES):
            index = half * C + k
            block = adj_recv.at[half, k]
            remote(block, block, a2s.at[index], a2r.at[index], k, p).wait_send()
            remote(block, block, a3s.at[index], a3r.at[index], k, p).wait_send()
        return carry

    lax.fori_loop(1, NB, end_facet, 0)
    lax.fori_loop(1, C, end_chan, 0)
    for copy in margin_copies + halo_copies:
        copy.wait_send()
    image_copy.wait()
    low_copy.wait()

    def end_wavelet(k, carry):
        pltpu.make_async_copy(wav.at[k], wavelet_out.at[k], wav_out_sem.at[k]).wait()
        return carry

    lax.fori_loop(0, C, end_wavelet, 0)
    data_copy.wait()


def hand_on(
    image_in, low_in, wavelet_in, data_in, image_out, low_out, wavelet_out, data_out, *scratch
):
    image, low, wavelet, data, sem_in, sem_out = scratch
    loads, stores = [], []
    for src, held, dst in (
        (wavelet_in, wavelet, wavelet_out),
        (image_in, image, image_out),
        (low_in, low, low_out),
        (data_in, data, data_out),
    ):
        for k in range(src.shape[0]):
            n = len(loads)
            loads.append(pltpu.make_async_copy(src.at[k], held.at[k], sem_in.at[n]))
            stores.append(pltpu.make_async_copy(held.at[k], dst.at[k], sem_out.at[n]))
    for copy in loads:
        copy.start()
    for load, store in zip(loads, stores):
        load.wait()
        store.start()
    for copy in stores:
        copy.wait()


def shards(
    image,
    lowrank_dual,
    wavelet_dual,
    data_dual,
    observed,
    kernel_weights,
    analysis_matrix,
    block_rows,
    intersection_widths,
    ball_radii,
):
    rows = R * BLK
    vmem = pltpu.VMEM
    dma = pltpu.SemaphoreType.DMA
    scratch = (
        [vmem((ROWS, 2 * N), bf16)] * 4
        + [
            vmem((2 * N, N), bf16),
            vmem((N, E), bf16),
            vmem((BLK, 2 * N), bf16),
            vmem((R, 2, NB, BLK), f32),
            vmem((C, E, 2 * E), f32),
            vmem((C, FS, E), f32),
            vmem((C, FS, E), f32),
            vmem((2, rows, BLK), f32),
            vmem((2, rows, BLK), f32),
            vmem((rows, BLK), bf16),
            vmem((E, R * E), bf16),
            vmem((NB, HALVES, HR, E), bf16),
            vmem((NB, HALVES, HR, E), bf16),
            vmem((CHUNKS, HR, ROWS), f32),
            vmem((HALVES, C, HR, E), bf16),
            vmem((HALVES, C, HR, E), bf16),
            vmem((E, E), bf16),
            vmem((E, E), bf16),
            vmem((C, E, E), bf16),
            vmem((4, E, FS), bf16),
            vmem((4, E, FS), bf16),
            vmem((C, FS, E), f32),
            vmem((C, HALO, E), bf16),
            vmem((C, HALO, E), bf16),
            vmem((4, HALO, FS), bf16),
            vmem((4, HALO, FS), bf16),
            vmem((4, HALO, FS), bf16),
            vmem((4, HALO, FS), bf16),
            vmem((4, FS, FS), bf16),
            vmem((4, FS, FS), bf16),
            vmem((4, FS, FS), bf16),
            vmem((4, FS, FS), bf16),
            vmem((C, E, E), bf16),
            vmem((4, FS, FS), bf16),
            vmem((4, FS, FS), bf16),
            vmem((4, E, FS), bf16),
            vmem((4, E, FS), bf16),
            vmem((HALVES, C, HR, E), bf16),
            vmem((HALVES, NB, HR, E), bf16),
            vmem((HALVES, NB, HR, E), bf16),
            vmem((rows, E), f32),
            vmem((C, C, FS), f32),
            vmem((C, C, FS), f32),
            vmem((C, FS, E), f32),
        ]
        + [dma((n,)) for n in (4, 4, 8, 7, 2, 8, 1)
            + (NB * HALVES,) * 2 + (C * HALVES,) * 4 + (NB * HALVES,) * 2 + (8,) * 4]
    )
    hbm = pl.BlockSpec(memory_space=pl.ANY)
    smem = pl.BlockSpec(memory_space=pltpu.SMEM)
    result_shapes = (
        jax.ShapeDtypeStruct((C, FS, E), f32),
        jax.ShapeDtypeStruct((C, FS, E), f32),
        jax.ShapeDtypeStruct((C, E, 2 * E), f32),
        jax.ShapeDtypeStruct((2, rows, BLK), f32),
    )
    results = pl.pallas_call(
        body,
        out_shape=result_shapes,
        in_specs=[smem] * 3 + [pl.BlockSpec(memory_space=pltpu.VMEM)] + [hbm] * 9,
        out_specs=(hbm,) * 4,
        scratch_shapes=scratch,
        compiler_params=pltpu.CompilerParams(
            collective_id=0, has_side_effects=True, vmem_limit_bytes=60 * 1024 * 1024
        ),
    )(
        block_rows,
        intersection_widths,
        ball_radii,
        analysis_matrix,
        image,
        lowrank_dual,
        wavelet_dual,
        data_dual.reshape(2, rows, BLK),
        observed.reshape(2, rows, BLK),
        kernel_weights.reshape(rows, BLK),
        jnp.asarray(dft_table()),
        jnp.asarray(first_row_table()),
        jnp.asarray(turned_table()),
    )
    image_next, lowrank_next, wavelet_next, data_next = pl.pallas_call(
        hand_on,
        out_shape=result_shapes,
        in_specs=[hbm] * 4,
        out_specs=(hbm,) * 4,
        scratch_shapes=[vmem(result.shape, f32) for result in result_shapes]
        + [dma((3 * C + 2,))] * 2,
        compiler_params=pltpu.CompilerParams(vmem_limit_bytes=60 * 1024 * 1024),
    )(*results)
    return image_next, lowrank_next, wavelet_next, data_next.reshape(2, 1, rows, BLK)


def solution(mesh):
    in_specs = (
        P(None, "facet", "chan"),
        P(None, "facet", "chan"),
        P(None, "facet", "chan"),
        P(None, "chan", None, "facet"),
        P(None, "chan", None, "facet"),
        P("chan", None, "facet"),
        P(),
        P("chan", "facet", None),
        P("facet", "chan"),
        P("chan", "facet"),
    )
    out_specs = (
        P(None, "facet", "chan"),
        P(None, "facet", "chan"),
        P(None, "facet", "chan"),
        P(None, "chan", None, "facet"),
    )
    return jax.shard_map(shards, mesh=mesh, in_specs=in_specs, out_specs=out_specs, check_vma=False)
```

```python
import math
from functools import partial

import jax
import jax.numpy as jnp
import ml_dtypes
import numpy as np
from jax import lax
from jax.experimental import pallas as pl
from jax.experimental.pallas import tpu as pltpu
from jax.sharding import PartitionSpec as P

N = 2048
FS = 128
HALO = 64
E = 256
BLK = 128
R = 4
C = 8
NB = 16
CHUNKS = 4
ROWS = N // CHUNKS
HALVES = 2
GROUP = 4
HR = FS // HALVES

step_size = 0.5
clip_bound = 1.5
shrink_ratio = 0.5
tiny_value = 1e-06

MESH = pl.DeviceIdType.MESH
f32 = jnp.float32
bf16 = jnp.bfloat16


def dft_table():
    index = np.arange(N, dtype=np.int64)
    angle = (index[:, None] * index[None, :] % N) * (2.0 * math.pi / N)
    scale = 1.0 / math.sqrt(N)
    parts = np.stack([np.cos(angle) * scale, -np.sin(angle) * scale])
    return (
        parts.reshape(2, N, NB, BLK)
        .transpose(1, 2, 0, 3)
        .reshape(N, 2 * N)
        .astype(ml_dtypes.bfloat16)
    )


def turned_table():
    return np.ascontiguousarray(dft_table().T)


def first_row_table():
    index = np.arange(N, dtype=np.int64)
    angle = (np.arange(BLK, dtype=np.int64)[:, None] * index[None, :] % N) * (2.0 * math.pi / N)
    scale = 1.0 / math.sqrt(N)
    parts = np.stack([np.cos(angle) * scale, -np.sin(angle) * scale])
    return (
        parts.reshape(2, BLK, NB // HALVES, HALVES, HALVES, HR)
        .transpose(1, 2, 4, 0, 3, 5)
        .reshape(BLK, 2 * N)
        .astype(ml_dtypes.bfloat16)
    )


def dot(a, b):
    return lax.dot_general(a, b, (((1,), (0,)), ((), ())), preferred_element_type=f32)


def dot_nt(a, b):
    return lax.dot_general(a, b, (((1,), (1,)), ((), ())), preferred_element_type=f32)


def swap_halves(x):
    return pltpu.roll(x, HALO, 1)


def lane_low(shape):
    return lax.broadcasted_iota(jnp.int32, shape, 1) < HALO


def facet_masks(width, up, down, left, right):
    row = lax.broadcasted_iota(jnp.int32, (E, FS), 0)
    away = jnp.maximum(jnp.maximum(HALO - row, row - (HALO + FS - 1)), 0)
    rows_in = (away <= width) & ((row >= HALO) | up) & ((row < HALO + FS) | down)
    lane = lax.broadcasted_iota(jnp.int32, (E, FS), 1)
    low = lane < HALO
    away = jnp.where(low, lane + 1, FS - lane)
    lanes_in = (away <= width) & ((low & right) | (jnp.logical_not(low) & left))
    return rows_in, rows_in & lanes_in


def body(
    rows_ref,
    widths_ref,
    radii_ref,
    matrix_ref,
    image_hbm,
    lowrank_hbm,
    wavelet_hbm,
    dual_hbm,
    observed_hbm,
    weights_hbm,
    table_hbm,
    row_table_hbm,
    turned_hbm,
    image_out,
    lowrank_out,
    wavelet_out,
    data_out,
    t0,
    t1,
    t2,
    t3,
    turned_rows,
    first_columns,
    first_rows,
    phases,
    wav,
    img,
    low,
    dual,
    obs,
    wgt,
    weighted,
    spread,
    rows_back,
    acc,
    adj_send,
    adj_recv,
    turned,
    rolled,
    syn,
    syn_left,
    syn_right,
    center,
    from_up,
    from_down,
    from_up_left,
    from_up_right,
    from_down_left,
    from_down_right,
    fold_left,
    fold_right,
    from_left,
    from_right,
    padded,
    edge_left,
    edge_right,
    halo_left,
    halo_right,
    regrouped,
    spec,
    spec_recv,
    forward,
    gram,
    shrink,
    low_next,
    table_sem,
    turned_sem,
    wav_sem,
    in_sem,
    out_sem,
    wav_out_sem,
    low_out_sem,
    a1s,
    a1r,
    a2s,
    a2r,
    a3s,
    a3r,
    a4s,
    a4r,
    h1s,
    h1r,
    h2s,
    h2r,
):
    tables = (t0, t1, t2, t3)
    c = lax.axis_index("chan")
    p = lax.axis_index("facet")
    up, down = lax.rem(p + NB - 1, NB), lax.rem(p + 1, NB)
    left, right = lax.rem(c + C - 1, C), lax.rem(c + 1, C)

    small = [
        pltpu.make_async_copy(src, dst, in_sem.at[k])
        for k, (src, dst) in enumerate(
            (
                (dual_hbm, dual),
                (weights_hbm, wgt),
                (image_hbm, img),
                (lowrank_hbm, low),
                (observed_hbm, obs),
            )
        )
    ]
    small[0].start()
    small[1].start()
    column_copy = pltpu.make_async_copy(
        table_hbm.at[pl.ds(0, N), pl.ds(0, E)], first_columns, in_sem.at[5]
    )
    column_copy.start()
    row_copy = pltpu.make_async_copy(row_table_hbm, first_rows, in_sem.at[6])
    table_copies = []
    for t in range(CHUNKS):
        copy = pltpu.make_async_copy(
            table_hbm.at[pl.ds(t * ROWS, ROWS)], tables[t], table_sem.at[t]
        )
        table_copies.append(copy)
    turned_copies = []
    for t in range(NB // GROUP):
        start = lax.rem(p // GROUP + t, NB // GROUP) * GROUP * E
        span = pl.ds(pl.multiple_of(start, GROUP * E), GROUP * E)
        turned_copies.append(
            pltpu.make_async_copy(turned_hbm.at[span], turned_rows.at[span], turned_sem.at[t])
        )

    barrier = pltpu.get_barrier_semaphore()

    def greet_facet(s, carry):
        peer = lax.rem(p + s, NB)
        pl.semaphore_signal(barrier, inc=1, device_id=(c, peer), device_id_type=MESH)
        return carry

    def greet_chan(s, carry):
        peer = lax.rem(c + s, C)
        pl.semaphore_signal(barrier, inc=1, device_id=(peer, p), device_id_type=MESH)
        return carry

    lax.fori_loop(1, NB, greet_facet, 0)
    lax.fori_loop(1, C, greet_chan, 0)

    matrix = matrix_ref[...]
    turned[...] = matrix.astype(f32).T.astype(bf16)
    rolled[...] = pltpu.roll(matrix.astype(f32), E - HALO, 1).astype(bf16)

    row16 = lax.broadcasted_iota(jnp.int32, (NB, BLK), 0)
    for q in range(R):
        turn = (rows_ref[0, 0, q] * row16) & (NB - 1)
        cosine, sine = jnp.zeros((NB, BLK), f32), jnp.zeros((NB, BLK), f32)
        for m in range(NB):
            cosine = jnp.where(turn == m, math.cos(2.0 * math.pi * m / NB), cosine)
            sine = jnp.where(turn == m, math.sin(2.0 * math.pi * m / NB), sine)
        phases[q, 0] = cosine
        phases[q, 1] = sine

    small[0].wait()
    small[1].wait()
    for q in range(R):
        span = slice(q * BLK, (q + 1) * BLK)
        weight = wgt[span, :].astype(f32)
        real = (dual[0, span, :] * weight).astype(bf16)
        imag = (dual[1, span, :] * weight).astype(bf16)
        lanes_real = slice(q * E, q * E + BLK)
        lanes_imag = slice(q * E + BLK, (q + 1) * E)
        weighted[:BLK, lanes_real] = real
        weighted[:BLK, lanes_imag] = imag
        weighted[BLK:, lanes_real] = imag
        weighted[BLK:, lanes_imag] = -real

    def remote(src, dst, send, recv, chan, facet):
        return pltpu.make_async_remote_copy(
            src_ref=src,
            dst_ref=dst,
            send_sem=send,
            recv_sem=recv,
            device_id=(chan, facet),
            device_id_type=MESH,
        )

    column_copy.wait()
    for k in range(C):
        pltpu.make_async_copy(wavelet_hbm.at[k], wav.at[k], wav_sem.at[k]).start()
    for copy in turned_copies:
        copy.start()
    for k in range(2, 5):
        small[k].start()
    for copy in table_copies:
        copy.start()
    row_copy.start()
    pl.semaphore_wait(barrier, NB - 1 + C - 1)

    def send_rows(target, half):
        remote(
            spread.at[target, half],
            rows_back.at[p, half],
            a1s.at[target * HALVES + half],
            a1r.at[p * HALVES + half],
            c,
            target,
        ).start()

    def spread_pair(s, carry):
        pair = lax.rem(p // 2 + s, NB // 2)
        start = pl.multiple_of(pair * 2 * FS, 2 * FS)
        out = dot(first_columns[pl.ds(start, 2 * FS), :], weighted[...])
        real, imag = None, None
        for q in range(R):
            part_real = out[:, q * E : q * E + BLK].reshape(16, NB, BLK)
            part_imag = out[:, q * E + BLK : (q + 1) * E].reshape(16, NB, BLK)
            cosine, sine = phases[q, 0][None], phases[q, 1][None]
            term_real = cosine * part_real - sine * part_imag
            term_imag = cosine * part_imag + sine * part_real
            real = term_real if real is None else real + term_real
            imag = term_imag if imag is None else imag + term_imag
        rounded = jnp.concatenate(
            [real.reshape(2 * FS, BLK), imag.reshape(2 * FS, BLK)], axis=1
        ).astype(bf16)
        for k in range(2):
            target = pair * 2 + k
            for half in range(HALVES):
                start = k * FS + half * HR
                spread[target, half] = rounded[start : start + HR]

            @pl.when(target != p)
            def _():
                send_rows(target, 0)

            @pl.when(target == p)
            def _():
                rows_back[p] = spread[target]

        return carry

    lax.fori_loop(1, NB // 2 + 1, spread_pair, 0)
    for half in range(1, HALVES):

        def send_later(s, carry):
            send_rows(lax.rem(p + s, NB), half)
            return carry

        lax.fori_loop(1, NB, send_later, 0)

    is_low = lane_low((E, FS))
    valid_up, valid_down = p > 0, p < NB - 1
    valid_left, valid_right = c > 0, c < C - 1

    def synth_channel(k, masks):
        pltpu.make_async_copy(wavelet_hbm.at[k], wav.at[k], wav_sem.at[k]).wait()
        half = dot(turned[...], wav[k].astype(bf16)).astype(bf16)
        cores, margins = [], []
        for f in range(2):
            out = dot(half[:, f * E : (f + 1) * E], rolled[...])
            rows_in, both = masks[f]
            cores.append(jnp.where(rows_in, out[:, :FS], 0.0))
            margins.append(jnp.where(both, out[:, FS:], 0.0))
        tile0 = cores[0] + jnp.where(is_low, 0.0, margins[1])
        tile1 = cores[1] + jnp.where(is_low, margins[0], 0.0)
        syn[k, :, :FS] = tile0.astype(bf16)
        syn[k, :, FS:] = tile1.astype(bf16)
        center[k, :, :FS] = tile0[HALO : HALO + FS]
        center[k, :, FS:] = tile1[HALO : HALO + FS]
        return margins

    true = p >= 0

    def synth_pair(k, carry):
        masks = [facet_masks(widths_ref[0, f], true, true, true, true) for f in range(2)]
        first = synth_channel(k, masks)
        second = synth_channel(k + 4, masks)
        syn_left[k] = jnp.where(is_low, swap_halves(second[0]), first[0]).astype(bf16)
        syn_right[k] = jnp.where(is_low, first[1], swap_halves(second[1])).astype(bf16)
        return carry

    lax.fori_loop(0, 4, synth_pair, 0)

    top, mid, bottom = pl.ds(0, HALO), pl.ds(HALO, FS), pl.ds(HALO + FS, HALO)
    every = slice(None)
    margin_copies = [
        remote(src, dst, h1s.at[k], h1r.at[k], a, b)
        for k, (src, dst, a, b) in enumerate(
            (
                (syn_left.at[every, top], from_down_left, c, up),
                (syn_left.at[every, bottom], from_up_left, c, down),
                (syn_right.at[every, top], from_down_right, c, up),
                (syn_right.at[every, bottom], from_up_right, c, down),
                (syn.at[every, top], from_down, c, up),
                (syn.at[every, bottom], from_up, c, down),
                (fold_left, from_right, left, p),
                (fold_right, from_left, right, p),
            )
        )
    ]
    to_up, to_down = (p > 0, p < NB - 1), (p < NB - 1, p > 0)
    to_left, to_right = (c > 0, c < C - 1), (c < C - 1, c > 0)
    margin_ends = [to_up, to_down] * 3 + [to_left, to_right]
    halo_ends = [to_left, to_right] + [to_up, to_down] * 3

    def start_some(copies, ends):
        for copy, (sends, _) in zip(copies, ends):

            @pl.when(sends)
            def _():
                copy.start()

    def receive_some(copies, ends):
        for copy, (_, receives) in zip(copies, ends):

            @pl.when(receives)
            def _():
                copy.wait_recv()

    def sent_some(copies, ends):
        for copy, (sends, _) in zip(copies, ends):

            @pl.when(sends)
            def _():
                copy.wait_send()

    start_some(margin_copies[:6], margin_ends[:6])

    for copy in turned_copies:
        copy.wait()

    def back_half(half):
        acc[...] = jnp.zeros_like(acc)

        def back_group(s, carry):
            g = lax.rem(p // GROUP + s, NB // GROUP)

            def arrive(k, carry):
                j = g * GROUP + k

                @pl.when(j != p)
                def _():
                    index = j * HALVES + half
                    block = rows_back.at[j, half]
                    remote(block, block, a1s.at[index], a1r.at[index], c, j).wait_recv()

                return carry

            lax.fori_loop(0, GROUP, arrive, 0)
            block = jnp.concatenate([rows_back[g * GROUP + k, half] for k in range(GROUP)], axis=1)
            start = pl.multiple_of(g * GROUP * E, GROUP * E)
            for t in range(CHUNKS):
                lanes = slice(t * ROWS, (t + 1) * ROWS)
                acc[t] += dot(block, turned_rows[pl.ds(start, GROUP * E), lanes])
            return carry

        lax.fori_loop(0, NB // GROUP, back_group, 0)
        for target in range(C):
            lanes = slice((target % 2) * E, (target % 2 + 1) * E)
            adj_send[half, target] = acc[target // 2, :, lanes].astype(bf16)

        def send_image(s, carry):
            target = lax.rem(c + s, C)
            remote(
                adj_send.at[half, target],
                adj_recv.at[half, c],
                a2s.at[half * C + target],
                a2r.at[half * C + c],
                target,
                p,
            ).start()
            return carry

        lax.fori_loop(1, C, send_image, 0)
        adj_recv[half, c] = adj_send[half, c]

    back_half(0)

    receive_some(margin_copies[:4], margin_ends[:4])
    row = lax.broadcasted_iota(jnp.int32, (FS, FS), 0)
    side_ok = ((row < HALO) & valid_up) | ((row >= HALO) & valid_down)

    def fold_edges(k, carry):
        for own, above, below, out in (
            (syn_left, from_up_left, from_down_left, fold_left),
            (syn_right, from_up_right, from_down_right, fold_right),
        ):
            beside = jnp.concatenate([above[k], below[k]], axis=0).astype(f32)
            total = own[k, HALO : HALO + FS].astype(f32) + jnp.where(side_ok, beside, 0.0)
            out[k] = total.astype(bf16)
        return carry

    lax.fori_loop(0, 4, fold_edges, 0)
    start_some(margin_copies[6:], margin_ends[6:])

    for half in range(1, HALVES):
        back_half(half)

    small[2].wait()
    small[3].wait()
    small[4].wait()
    receive_some(margin_copies[4:], margin_ends[4:])
    half_low = lane_low((FS, FS))

    def gather_prior(k, carry):
        pair = lax.rem(k, 4)
        is_first = k < 4
        sides = from_left[pair].astype(f32)
        sides = jnp.where(is_first, sides, swap_halves(sides))
        tile0 = jnp.where(half_low & valid_left, sides, 0.0)
        sides = from_right[pair].astype(f32)
        sides = jnp.where(is_first, sides, swap_halves(sides))
        tile1 = jnp.where(jnp.logical_not(half_low) & valid_right, sides, 0.0)
        above = jnp.where(valid_up, from_up[k].astype(f32), 0.0)
        below = jnp.where(valid_down, from_down[k].astype(f32), 0.0)
        sides = jnp.concatenate([tile0, tile1], axis=1)
        vertical = jnp.concatenate([above, below], axis=0)
        prior = center[k] + sides + vertical
        center[k] = img[k] - step_size * (prior + low[k])
        return carry

    lax.fori_loop(0, C, gather_prior, 0)

    def image_half(half):
        inside = slice(half * HR, (half + 1) * HR)
        here = pl.ds(HALO + half * HR, HR)

        def image_step(s, carry):
            k = lax.rem(c + s, C)

            @pl.when(s > 0)
            def _():
                index = half * C + k
                block = adj_recv.at[half, k]
                remote(block, block, a2s.at[index], a2r.at[index], k, p).wait_recv()

            adjoint = adj_recv[half, k].astype(f32)
            updated = jnp.maximum(center[k, inside] - step_size * adjoint, 0.0)
            tilde = 2.0 * updated - img[k, inside]
            center[k, inside] = updated
            padded[k, here] = tilde.astype(bf16)
            low[k, inside] = low[k, inside] + tilde

            @pl.when(s > 0)
            def _():
                remote(
                    padded.at[k, here],
                    regrouped.at[half, c],
                    a3s.at[half * C + k],
                    a3r.at[half * C + c],
                    k,
                    p,
                ).start()

            @pl.when(s == 0)
            def _():
                regrouped[half, c] = tilde.astype(bf16)

            return carry

        lax.fori_loop(0, C, image_step, 0)

    for half in range(HALVES):
        image_half(half)
    image_copy = pltpu.make_async_copy(center, image_out, out_sem.at[0])
    image_copy.start()

    def pack_edges(k, carry):
        first = padded[k, HALO : HALO + FS, :].astype(f32)
        second = padded[k + 4, HALO : HALO + FS, :].astype(f32)
        edge_right[k] = jnp.where(
            half_low, swap_halves(second[:, FS:]), first[:, FS:]
        ).astype(bf16)
        edge_left[k] = jnp.where(
            half_low, first[:, :FS], swap_halves(second[:, :FS])
        ).astype(bf16)
        return carry

    lax.fori_loop(0, 4, pack_edges, 0)
    upper, lower = pl.ds(HALO, HALO), pl.ds(FS, HALO)
    halo_copies = [
        remote(src, dst, h2s.at[k], h2r.at[k], a, b)
        for k, (src, dst, a, b) in enumerate(
            (
                (edge_left, halo_right.at[every, mid], left, p),
                (edge_right, halo_left.at[every, mid], right, p),
                (padded.at[every, upper], padded.at[every, bottom], c, up),
                (padded.at[every, lower], padded.at[every, top], c, down),
                (halo_left.at[every, upper], halo_left.at[every, bottom], c, up),
                (halo_left.at[every, lower], halo_left.at[every, top], c, down),
                (halo_right.at[every, upper], halo_right.at[every, bottom], c, up),
                (halo_right.at[every, lower], halo_right.at[every, top], c, down),
            )
        )
    ]
    start_some(halo_copies[:4], halo_ends[:4])

    def spectrum_half(half):
        def arrive(s, carry):
            k = lax.rem(c + s, C)
            index = half * C + k
            block = regrouped.at[half, k]
            remote(block, block, a3s.at[index], a3r.at[index], k, p).wait_recv()
            return carry

        lax.fori_loop(1, C, arrive, 0)

        def spectrum_block(s, carry):
            j = lax.rem(p + s, NB)
            start = pl.multiple_of(j * E, E)
            total = None
            for q in range(C):
                rows_in = slice((q % 2) * E, (q % 2 + 1) * E)
                term = dot(regrouped[half, q], tables[q // 2][rows_in, pl.ds(start, E)])
                total = term if total is None else total + term
            spec[half, j] = total.astype(bf16)

            @pl.when(s < NB)
            def _():
                remote(
                    spec.at[half, j],
                    spec_recv.at[half, p],
                    a4s.at[half * NB + j],
                    a4r.at[half * NB + p],
                    c,
                    j,
                ).start()

            @pl.when(s == NB)
            def _():
                spec_recv[half, p] = total.astype(bf16)

            return carry

        lax.fori_loop(1, NB + 1, spectrum_block, 0)

    for copy in table_copies:
        copy.wait()
    spectrum_half(0)
    receive_some(halo_copies[:2], halo_ends[:2])
    start_some(halo_copies[4:], halo_ends[4:])
    for half in range(1, HALVES):
        spectrum_half(half)

    for f in range(2):
        lanes = slice(f * FS, (f + 1) * FS)

        def gram_row(a, carry):
            mine = low[a, :, lanes].astype(bf16).astype(f32)
            for b in range(C):
                other = low[b, :, lanes].astype(bf16).astype(f32)
                gram[a, b : b + 1, :] = jnp.sum(mine * other, axis=0, keepdims=True)
            return carry

        lax.fori_loop(0, C, gram_row, 0)
        total = jnp.sum(gram[...], axis=2)
        row = lax.broadcasted_iota(jnp.int32, (C, C), 0)
        col = lax.broadcasted_iota(jnp.int32, (C, C), 1)
        eye = (row == col).astype(f32)
        trace = jnp.sum(jnp.sum(total * eye, axis=1, keepdims=True), axis=0, keepdims=True)
        ridge = shrink_ratio * (trace / C + tiny_value)
        system = total + ridge * eye
        inverse = eye
        for k in range(C):
            pivot = 1.0 / system[k : k + 1, k : k + 1]
            row_s = system[k : k + 1, :] * pivot
            row_i = inverse[k : k + 1, :] * pivot
            column = jnp.where(row == k, 0.0, jnp.broadcast_to(system[:, k : k + 1], (C, C)))
            system = jnp.where(row == k, jnp.broadcast_to(row_s, (C, C)), system - column * row_s)
            inverse = jnp.where(row == k, jnp.broadcast_to(row_i, (C, C)), inverse - column * row_i)
        inverse = ridge * inverse
        for k in range(C):
            shrink[k] = jnp.broadcast_to(inverse[:, k : k + 1], (C, FS))

        def apply_row(r, carry):
            span = pl.ds(pl.multiple_of(r * 16, 16), 16)
            blocks = [low[b, span, lanes] for b in range(C)]
            for a in range(C):
                out = None
                for b in range(C):
                    term = shrink[b, a : a + 1, :] * blocks[b]
                    out = term if out is None else out + term
                low_next[a, span, lanes] = out
            return carry

        lax.fori_loop(0, FS // 16, apply_row, 0)
    low_copy = pltpu.make_async_copy(low_next, lowrank_out, low_out_sem.at[0])
    low_copy.start()

    receive_some(halo_copies[2:], halo_ends[2:])

    def analysis(k, carry):
        pair = lax.rem(k, 4)
        is_first = k < 4
        tiles = padded[k].astype(f32)
        tile0, tile1 = tiles[:, :FS], tiles[:, FS:]
        side = halo_left[pair].astype(f32)
        beside_left = jnp.where(is_first, side, swap_halves(side))
        side = halo_right[pair].astype(f32)
        beside_right = jnp.where(is_first, side, swap_halves(side))
        margins = (
            jnp.where(is_low, tile1, beside_left),
            jnp.where(is_low, beside_right, tile0),
        )
        for f in range(2):
            rows_in, both = facet_masks(
                widths_ref[0, f],
                valid_up,
                valid_down,
                valid_left if f == 0 else true,
                valid_right if f == 1 else true,
            )
            core = jnp.where(rows_in, tile0 if f == 0 else tile1, 0.0)
            margin = jnp.where(both, margins[f], 0.0)
            piece = jnp.concatenate([core, margin], axis=1).astype(bf16)
            half = dot(matrix_ref[...], piece).astype(bf16)
            coefficients = dot_nt(half, rolled[...])
            lanes = slice(f * E, (f + 1) * E)
            wav[k, :, lanes] = jnp.clip(wav[k, :, lanes] + coefficients, -clip_bound, clip_bound)
        pltpu.make_async_copy(wav.at[k], wavelet_out.at[k], wav_out_sem.at[k]).start()
        return carry

    lax.fori_loop(0, C, analysis, 0)

    forward[...] = jnp.zeros_like(forward)
    row_copy.wait()

    def forward_block(s, carry):
        half = s // (NB // HALVES)
        g = lax.rem(p // HALVES + s, NB // HALVES)
        for b in range(HALVES):
            j = g * HALVES + b

            @pl.when(j != p)
            def _():
                index = half * NB + j
                block = spec_recv.at[half, j]
                remote(block, block, a4s.at[index], a4r.at[index], c, j).wait_recv()

        block = jnp.concatenate(
            [spec_recv[half, g * HALVES + b].astype(f32) for b in range(HALVES)], axis=0
        )
        real = block[:, :BLK].reshape(FS // NB, NB, BLK)
        imag = block[:, BLK:].reshape(FS // NB, NB, BLK)
        start = pl.multiple_of((g * HALVES + half) * E, E)
        rows_table = first_rows[:, pl.ds(start, E)]
        for q in range(R):
            cosine, sine = phases[q, 0][None], phases[q, 1][None]
            turned_real = (cosine * real + sine * imag).reshape(FS, BLK)
            turned_imag = (cosine * imag - sine * real).reshape(FS, BLK)
            upper_rows = jnp.concatenate([turned_real, turned_imag], axis=1)
            lower_rows = jnp.concatenate([-turned_imag, turned_real], axis=1)
            both = jnp.concatenate([upper_rows, lower_rows], axis=0).astype(bf16)
            forward[q * BLK : (q + 1) * BLK, :] += dot(rows_table, both)
        return carry

    lax.fori_loop(0, NB, forward_block, 0)

    weight = wgt[...].astype(f32)
    squares = jnp.zeros((1, BLK), f32)
    for part in range(2):
        residual = dual[part] + weight * forward[:, part * BLK : (part + 1) * BLK] - obs[part]
        dual[part] = residual
        squares = squares + jnp.sum(residual * residual, axis=0, keepdims=True)
    norm = jnp.sqrt(jnp.sum(squares, axis=1, keepdims=True))
    radius = radii_ref[0, 0]
    factor = jnp.maximum(0.0, 1.0 - radius / jnp.maximum(norm, radius))
    for part in range(2):
        dual[part] = dual[part] * factor
    data_copy = pltpu.make_async_copy(dual, data_out, out_sem.at[1])
    data_copy.start()

    def end_facet(s, carry):
        j = lax.rem(p + s, NB)
        for half in range(HALVES):
            block = spec_recv.at[half, j]
            sem = a1s.at[j * HALVES + half]
            remote(block, block, sem, a1r.at[0], c, j).wait_send()
            sem = a4s.at[half * NB + j]
            remote(block, block, sem, a4r.at[0], c, j).wait_send()
        return carry

    def end_chan(s, carry):
        k = lax.rem(c + s, C)
        for half in range(HALVES):
            index = half * C + k
            block = adj_recv.at[half, k]
            remote(block, block, a2s.at[index], a2r.at[index], k, p).wait_send()
            remote(block, block, a3s.at[index], a3r.at[index], k, p).wait_send()
        return carry

    lax.fori_loop(1, NB, end_facet, 0)
    lax.fori_loop(1, C, end_chan, 0)
    sent_some(margin_copies + halo_copies, margin_ends + halo_ends)
    image_copy.wait()
    low_copy.wait()

    def end_wavelet(k, carry):
        pltpu.make_async_copy(wav.at[k], wavelet_out.at[k], wav_out_sem.at[k]).wait()
        return carry

    lax.fori_loop(0, C, end_wavelet, 0)
    data_copy.wait()


def hand_on(
    image_in, low_in, wavelet_in, data_in, image_out, low_out, wavelet_out, data_out, *scratch
):
    image, low, wavelet, data, sem_in, sem_out = scratch
    loads, stores = [], []
    for src, held, dst in (
        (wavelet_in, wavelet, wavelet_out),
        (image_in, image, image_out),
        (low_in, low, low_out),
        (data_in, data, data_out),
    ):
        for k in range(src.shape[0]):
            n = len(loads)
            loads.append(pltpu.make_async_copy(src.at[k], held.at[k], sem_in.at[n]))
            stores.append(pltpu.make_async_copy(held.at[k], dst.at[k], sem_out.at[n]))
    for copy in loads:
        copy.start()
    for load, store in zip(loads, stores):
        load.wait()
        store.start()
    for copy in stores:
        copy.wait()


def shards(
    image,
    lowrank_dual,
    wavelet_dual,
    data_dual,
    observed,
    kernel_weights,
    analysis_matrix,
    block_rows,
    intersection_widths,
    ball_radii,
):
    rows = R * BLK
    vmem = pltpu.VMEM
    dma = pltpu.SemaphoreType.DMA
    scratch = (
        [vmem((ROWS, 2 * N), bf16)] * 4
        + [
            vmem((2 * N, N), bf16),
            vmem((N, E), bf16),
            vmem((BLK, 2 * N), bf16),
            vmem((R, 2, NB, BLK), f32),
            vmem((C, E, 2 * E), f32),
            vmem((C, FS, E), f32),
            vmem((C, FS, E), f32),
            vmem((2, rows, BLK), f32),
            vmem((2, rows, BLK), f32),
            vmem((rows, BLK), bf16),
            vmem((E, R * E), bf16),
            vmem((NB, HALVES, HR, E), bf16),
            vmem((NB, HALVES, HR, E), bf16),
            vmem((CHUNKS, HR, ROWS), f32),
            vmem((HALVES, C, HR, E), bf16),
            vmem((HALVES, C, HR, E), bf16),
            vmem((E, E), bf16),
            vmem((E, E), bf16),
            vmem((C, E, E), bf16),
            vmem((4, E, FS), bf16),
            vmem((4, E, FS), bf16),
            vmem((C, FS, E), f32),
            vmem((C, HALO, E), bf16),
            vmem((C, HALO, E), bf16),
            vmem((4, HALO, FS), bf16),
            vmem((4, HALO, FS), bf16),
            vmem((4, HALO, FS), bf16),
            vmem((4, HALO, FS), bf16),
            vmem((4, FS, FS), bf16),
            vmem((4, FS, FS), bf16),
            vmem((4, FS, FS), bf16),
            vmem((4, FS, FS), bf16),
            vmem((C, E, E), bf16),
            vmem((4, FS, FS), bf16),
            vmem((4, FS, FS), bf16),
            vmem((4, E, FS), bf16),
            vmem((4, E, FS), bf16),
            vmem((HALVES, C, HR, E), bf16),
            vmem((HALVES, NB, HR, E), bf16),
            vmem((HALVES, NB, HR, E), bf16),
            vmem((rows, E), f32),
            vmem((C, C, FS), f32),
            vmem((C, C, FS), f32),
            vmem((C, FS, E), f32),
        ]
        + [dma((n,)) for n in (4, 4, 8, 7, 2, 8, 1)
            + (NB * HALVES,) * 2 + (C * HALVES,) * 4 + (NB * HALVES,) * 2 + (8,) * 4]
    )
    hbm = pl.BlockSpec(memory_space=pl.ANY)
    smem = pl.BlockSpec(memory_space=pltpu.SMEM)
    result_shapes = (
        jax.ShapeDtypeStruct((C, FS, E), f32),
        jax.ShapeDtypeStruct((C, FS, E), f32),
        jax.ShapeDtypeStruct((C, E, 2 * E), f32),
        jax.ShapeDtypeStruct((2, rows, BLK), f32),
    )
    results = pl.pallas_call(
        body,
        out_shape=result_shapes,
        in_specs=[smem] * 3 + [pl.BlockSpec(memory_space=pltpu.VMEM)] + [hbm] * 9,
        out_specs=(hbm,) * 4,
        scratch_shapes=scratch,
        compiler_params=pltpu.CompilerParams(
            collective_id=0, has_side_effects=True, vmem_limit_bytes=60 * 1024 * 1024
        ),
    )(
        block_rows,
        intersection_widths,
        ball_radii,
        analysis_matrix,
        image,
        lowrank_dual,
        wavelet_dual,
        data_dual.reshape(2, rows, BLK),
        observed.reshape(2, rows, BLK),
        kernel_weights.reshape(rows, BLK),
        jnp.asarray(dft_table()),
        jnp.asarray(first_row_table()),
        jnp.asarray(turned_table()),
    )
    image_next, lowrank_next, wavelet_next, data_next = pl.pallas_call(
        hand_on,
        out_shape=result_shapes,
        in_specs=[hbm] * 4,
        out_specs=(hbm,) * 4,
        scratch_shapes=[vmem(result.shape, f32) for result in result_shapes]
        + [dma((3 * C + 2,))] * 2,
        compiler_params=pltpu.CompilerParams(vmem_limit_bytes=60 * 1024 * 1024),
    )(*results)
    return image_next, lowrank_next, wavelet_next, data_next.reshape(2, 1, rows, BLK)


def solution(mesh):
    in_specs = (
        P(None, "facet", "chan"),
        P(None, "facet", "chan"),
        P(None, "facet", "chan"),
        P(None, "chan", None, "facet"),
        P(None, "chan", None, "facet"),
        P("chan", None, "facet"),
        P(),
        P("chan", "facet", None),
        P("facet", "chan"),
        P("chan", "facet"),
    )
    out_specs = (
        P(None, "facet", "chan"),
        P(None, "facet", "chan"),
        P(None, "facet", "chan"),
        P(None, "chan", None, "facet"),
    )
    return jax.shard_map(shards, mesh=mesh, in_specs=in_specs, out_specs=out_specs, check_vma=False)
```
